512 devices in a mesh: row: 16 (over y, z_hi), col: 32 (over z_lo, x, core).
Axes of the slice: x: 4, y: 4, z: 16 (z_hi: 4, z_lo: 4; z = z_hi * 4 + z_lo), core: 2. Of those that a mesh axis runs over, the one named last changes fastest.
Arguments:
- features: bfloat16 [65536, 256], P(('col', 'row')), may hold values from -6 to 6
- weight: bfloat16 [256, 256], replicated, may hold values from -0.375 to 0.375
- tiles: bfloat16 [16, 32, 96, 128, 128], P('row', 'col'), may hold values from -0.09375 to 0.09375
- coords: int32 [16, 32, 96, 2], P('row', 'col'), may hold values from 0 to 31, as said below
- counts: int32 [16, 32], P('row', 'col'), may hold values from 12 to 96, as said below
- cotangent: bfloat16 [65536, 256], P(('row', 'col')), may hold values from -6 to 6
Outputs:
- output: bfloat16 [65536, 256], P(('row', 'col'))
- grad_features: bfloat16 [65536, 256], P(('col', 'row'))
- grad_weight: float32 [256, 256], replicated
The draws below stay inside these ranges and needn't reach their ends.
Inputs may be any that keep to these rules, and one draw needn't show every extreme that they name: `coords`: within one device the slots name distinct tile positions; the first entry is below 32, the second below 16. `counts`: some device has all 96 slots live in every draw.
All inputs are finite; a program needn't handle non-finite values.
Results may differ from the reference program's by a relative error of at most 0.017.
Values may be sent and summed in bfloat16 or wider, within the bound.
A program may use at most 64 MiB of HBM per device.

```python
import jax
import jax.numpy as jnp
from jax import lax

HID = 256
TILE = 128
NODES = 65536
TROWS = 32
TCOLS = 16
SLOTS = 96
N_ROW = 16
N_COL = 32


def draw_coords(key, part):
    key = jax.random.fold_in(key, 11)
    keys = jax.random.split(key, N_ROW * N_COL)

    def single(sub):
        chosen = jax.random.permutation(sub, TROWS * TCOLS)[:SLOTS].astype(jnp.int32)
        return jnp.stack([chosen // TCOLS, chosen % TCOLS], -1)
    return jax.vmap(single)(keys).reshape(N_ROW, N_COL, SLOTS, 2).astype(jnp.int32)


def draw_counts(key, part):
    key = jax.random.fold_in(key, 23)
    first, second, third = jax.random.split(key, 3)
    lower = max(1, SLOTS // 8)
    base = jax.random.randint(first, (N_ROW, N_COL), lower, SLOTS // 2 + 1)
    busy = jax.random.randint(second, (N_ROW, N_COL), 0, 16) == 0
    chosen = jax.random.randint(third, (), 0, N_ROW * N_COL)
    forced = jnp.arange(N_ROW * N_COL).reshape(N_ROW, N_COL) == chosen
    return jnp.where(busy | forced, SLOTS, base).astype(jnp.int32)


def levels(own_key, dims, shards, least, high):
    def one(dim, shards_of):
        heights = jax.random.uniform(jax.random.fold_in(jax.random.fold_in(own_key, 6), dim), (shards_of,), jnp.float32, least / len(shards), high / len(shards))
        return jnp.repeat(jnp.exp(heights), dims[dim] // shards_of).reshape((-1,) + (1,) * (len(dims) - dim - 1))

    level = one(*shards[0])
    for cut in shards[1:]:
        level = level * one(*cut)
    return level


def centred(rng, dims, scale, most, pieces=(), held_as=jnp.bfloat16):
    drawn = scale * jax.random.normal(rng, dims, jnp.float32)
    if pieces:
        drawn = drawn * levels(rng, dims, pieces, -0.22, 0.18)
    return jnp.clip(drawn, -most, most).astype(held_as)


def setup_inputs(seed: int = 0) -> dict:
    splits = jax.random.split(jax.random.key(seed), 7)
    return {
        "features": centred(splits[0], (NODES, HID), 1.0, 6.0, ((0, 512),)),
        "weight": centred(splits[1], (HID, HID), HID ** -0.5, 0.375),
        "tiles": centred(splits[2], (N_ROW, N_COL, SLOTS, TILE, TILE), (N_COL * SLOTS * TILE // (3 * TROWS)) ** -0.5, 0.09375, ((0, 16), (1, 32))),
        "coords": draw_coords(jax.random.fold_in(splits[6], 71), 0),
        "counts": draw_counts(jax.random.fold_in(splits[6], 71), 0),
        "cotangent": centred(splits[5], (NODES, HID), 1.0, 6.0, ((0, 512),)),
    }


def silu_slope(hidden):
    sig = jax.nn.sigmoid(hidden)
    return sig * (1.0 + hidden * (1.0 - sig))


def reference(features, weight, tiles, coords, counts, cotangent):
    projected = jnp.dot(features, weight, preferred_element_type=jnp.float32).astype(jnp.bfloat16)
    proj_tiles = projected.reshape(NODES // TILE, TILE, HID)
    flat_tiles = tiles.reshape(N_ROW * N_COL, SLOTS, TILE, TILE)
    flat_coords = coords.reshape(N_ROW * N_COL, SLOTS, 2)
    flat_counts = counts.reshape(N_ROW * N_COL)
    device_ids = jnp.arange(N_ROW * N_COL, dtype=jnp.int32)
    slot_ids = jnp.arange(SLOTS, dtype=jnp.int32)

    def places(device, dev_coords, dev_count):
        grow = (device // N_COL) * TROWS + dev_coords[:, 0]
        gcol = (device % N_COL) * TCOLS + dev_coords[:, 1]
        live = (slot_ids < dev_count).astype(jnp.float32)
        return grow.astype(jnp.int32), gcol.astype(jnp.int32), live

    def forward_step(total, inputs):
        dev_tiles, dev_coords, dev_count, device = inputs
        grow, gcol, live = places(device, dev_coords, dev_count)
        panel = proj_tiles[gcol].astype(jnp.float32)
        prod = jnp.einsum("sij,sjh->sih", dev_tiles.astype(jnp.float32), panel) * live[:, None, None]
        return total.at[grow].add(prod), None

    start = jnp.zeros((NODES // TILE, TILE, HID), jnp.float32)
    total, _ = lax.scan(forward_step, start, (flat_tiles, flat_coords, flat_counts, device_ids))
    hidden = total.reshape(NODES, HID)
    output = jax.nn.silu(hidden).astype(jnp.bfloat16)
    grad_hidden = (cotangent.astype(jnp.float32) * silu_slope(hidden)).astype(jnp.bfloat16)
    grad_tiles = grad_hidden.reshape(NODES // TILE, TILE, HID)

    def backward_step(total, inputs):
        dev_tiles, dev_coords, dev_count, device = inputs
        grow, gcol, live = places(device, dev_coords, dev_count)
        panel = grad_tiles[grow].astype(jnp.float32)
        prod = jnp.einsum("sji,sjh->sih", dev_tiles.astype(jnp.float32), panel) * live[:, None, None]
        return total.at[gcol].add(prod), None

    back_total, _ = lax.scan(backward_step, start, (flat_tiles, flat_coords, flat_counts, device_ids))
    grad_projected = back_total.reshape(NODES, HID).astype(jnp.bfloat16)
    grad_features = jnp.dot(grad_projected, weight.T, preferred_element_type=jnp.float32).astype(jnp.bfloat16)
    grad_weight = jnp.dot(features.T, grad_projected, preferred_element_type=jnp.float32)
    return output, grad_features, grad_weight
```

```python
import functools

import jax
import jax.numpy as jnp
from jax import lax
from jax.experimental import pallas as pl
from jax.experimental.pallas import tpu as pltpu
from jax.sharding import PartitionSpec as P

F32 = jnp.float32
BF16 = jnp.bfloat16
MESH = pl.DeviceIdType.MESH
TILE = 128
HID = 256
TROWS = 32
TCOLS = 16
SLOTS = 96
GROUP = 16
UNROLL = 4
VMEM_LIMIT = 28 * 2**20
LOW = slice(0, 64)
HIGH = slice(64, 128)


def flip1(v):
    return v + 1 - 2 * lax.rem(v, 2)


def flip2(v):
    return lax.rem(v + 2, 4)


def flip3(v):
    return 3 - v


FLIPS = {0: lambda v: v, 1: flip1, 2: flip2, 3: flip3}


class Place:
    def __init__(self):
        row = lax.axis_index("row")
        col = lax.axis_index("col")
        self.y = lax.div(row, 4)
        self.zh = lax.rem(row, 4)
        self.zl = lax.div(col, 8)
        self.x = lax.rem(lax.div(col, 2), 4)
        self.core = lax.rem(col, 2)

    def peer(self, y=0, zh=0, zl=0, x=0, core=0):
        row = FLIPS[y](self.y) * 4 + FLIPS[zh](self.zh)
        col = FLIPS[zl](self.zl) * 8 + FLIPS[x](self.x) * 2 + FLIPS[core](self.core)
        return (row, col)


class Net:
    def __init__(self, send_sems, recv_sems):
        self.send_sems = send_sems
        self.recv_sems = recv_sems
        self.started = []

    def send(self, src, dst, device):
        i = len(self.started)
        copy = pltpu.make_async_remote_copy(
            src_ref=src,
            dst_ref=dst,
            send_sem=self.send_sems.at[i],
            recv_sem=self.recv_sems.at[i],
            device_id=device,
            device_id_type=MESH,
        )
        copy.start()
        self.started.append(copy)
        return copy

    def finish(self):
        for copy in self.started:
            copy.wait_send()


def greet(peers):
    barrier = pltpu.get_barrier_semaphore()
    for peer in peers:
        pl.semaphore_signal(barrier, inc=1, device_id=peer, device_id_type=MESH)
    pl.semaphore_wait(barrier, len(peers))


def add(*values):
    total = values[0].astype(F32)
    for value in values[1:]:
        total = total + value.astype(F32)
    return total.astype(BF16)


def ring_gather(net, at, near, far):
    copies = {}

    def first():
        copies["n"] = net.send(at(0, None), at(1, None), near)
        copies["f"] = net.send(at(0, None), at(3, None), far)

    def second():
        copies["n"].wait_recv()
        copies["nf"] = net.send(at(1, LOW), at(2, LOW), far)
        copies["f"].wait_recv()
        copies["fn"] = net.send(at(3, HIGH), at(2, HIGH), near)

    def third():
        copies["nf"].wait_recv()
        copies["fn"].wait_recv()

    return first, second, third


def ring_scatter(net, at, landing, near, far):
    copies = {}

    def first():
        copies["t1"] = net.send(at(2, LOW), landing.at[2, LOW], near)
        copies["t3"] = net.send(at(2, HIGH), landing.at[2, HIGH], far)
        copies["n0"] = net.send(at(1, LOW), landing.at[0, LOW], near)
        copies["f1"] = net.send(at(3, HIGH), landing.at[1, HIGH], far)

    def second():
        copies["t1"].wait_recv()
        share = at(3, LOW)
        share[...] = add(share[...], landing[2, LOW])
        copies["f0"] = net.send(share, landing.at[1, LOW], far)
        copies["t3"].wait_recv()
        share = at(1, HIGH)
        share[...] = add(share[...], landing[2, HIGH])
        copies["n1"] = net.send(share, landing.at[0, HIGH], near)

    def third():
        for name in ("n0", "f1", "f0", "n1"):
            copies[name].wait_recv()

    return first, second, third


def gather_kernel(features, weight, panel, send_sems, recv_sems):
    place = Place()
    net = Net(send_sems, recv_sems)
    z_near, z_far = place.peer(zh=1), place.peer(zh=3)
    y_near, y_far = place.peer(y=1), place.peer(y=3)
    panel[0, 0] = jnp.dot(features[...], weight[...], preferred_element_type=F32).astype(BF16)
    greet((z_near, z_far, y_near, y_far))

    def at_z(i, rows):
        return panel.at[0, i] if rows is None else panel.at[0, i, rows]

    def at_y(k):
        return lambda i, rows: panel.at[i, k] if rows is None else panel.at[i, k, rows]

    z1, z2, z3 = ring_gather(net, at_z, z_near, z_far)
    rings = [ring_gather(net, at_y(k), y_near, y_far) for k in range(4)]
    z1()
    rings[0][0]()
    rings[0][1]()
    z2()
    rings[1][0]()
    rings[3][0]()
    rings[1][1]()
    rings[3][1]()
    z3()
    rings[2][0]()
    rings[2][1]()
    for k in (0, 1, 3, 2):
        rings[k][2]()
    net.finish()


def products_kernel(back, enc, count, tiles, panel, out, held, acc, sems):
    live = count[0, 0]
    groups = SLOTS // GROUP
    targets = TCOLS if back else TROWS

    def fetch(g):
        part = pl.ds(g * GROUP, GROUP)
        return pltpu.make_async_copy(tiles.at[part], held.at[part], sems.at[g])

    for g in range(groups):
        @pl.when(g * GROUP < live)
        def _():
            fetch(g).start()

    def clear(t, carry):
        acc[t] = jnp.zeros((TILE, HID), F32)
        return carry

    lax.fori_loop(0, targets, clear, 0)

    def product(slot):
        code = enc[slot]
        first, second = lax.shift_right_logical(code, 4), lax.bitwise_and(code, 15)
        target, source = (second, first) if back else (first, second)
        target = jnp.where(slot < live, target, targets)
        dims = (((0,), (0,)), ((), ())) if back else (((1,), (0,)), ((), ()))
        value = lax.dot_general(held[slot], panel[source], dims, preferred_element_type=F32)
        return target, value

    for g in range(groups):
        @pl.when(g * GROUP < live)
        def _():
            fetch(g).wait()

            def step(i, carry):
                base = g * GROUP + i * UNROLL
                done = [product(base + u) for u in range(UNROLL)]
                for target, value in done:
                    acc[target] += value
                return carry

            steps = lax.min(lax.div(live - g * GROUP + UNROLL - 1, UNROLL), GROUP // UNROLL)
            lax.fori_loop(0, steps, step, 0)

    def pack(t, carry):
        out[t] = acc[t].astype(BF16)
        return carry

    lax.fori_loop(0, targets, pack, 0)


def middle_kernel(
    partial, cotangent, output, grads, from_core, from_x, total, from_z, send_sems, recv_sems
):
    place = Place()
    net = Net(send_sems, recv_sems)
    other = place.peer(core=1)
    near, far = place.peer(x=1), place.peer(x=3)
    along = {k: place.peer(zl=k) for k in (1, 2, 3)}
    greet((other, near, far, along[1], along[2], along[3]))
    order = (3, 2, 1, 0)

    core_copies = {
        k: net.send(partial.at[k, :, 1], from_core.at[k], other) for k in order
    }

    def at_x(k):
        return lambda i, rows: from_core.at[k, i, rows]

    rings = {k: ring_scatter(net, at_x(k), from_x.at[k], near, far) for k in order}
    z_copies = {}

    def start(k):
        core_copies[k].wait_recv()
        for i in (2, 1, 3):
            from_core[k, i] = add(from_core[k, i], partial[k, i, 0])
        rings[k][0]()

    def close(k):
        rings[k][2]()
        parts = (partial[k, 0, 0], from_core[k, 0], from_x[k, 0], from_x[k, 1])
        if k:
            total[k] = add(*parts)
            z_copies[k] = net.send(total.at[k], from_z.at[k], along[k])
            return None
        return sum(part.astype(F32) for part in parts)

    start(3)
    start(2)
    rings[3][1]()
    start(1)
    rings[2][1]()
    close(3)
    start(0)
    rings[1][1]()
    close(2)
    rings[0][1]()
    close(1)
    hidden = close(0)
    for k in (3, 2, 1):
        z_copies[k].wait_recv()
        hidden = hidden + from_z[k].astype(F32)
    sig = jax.nn.sigmoid(hidden)
    slope = sig * (1.0 + hidden * (1.0 - sig))
    grads[0, 0, 0] = (cotangent[...].astype(F32) * slope).astype(BF16)

    out_copies = {k: net.send(grads.at[0, 0, 0], grads.at[k, 0, 0], along[k]) for k in (1, 2, 3)}

    def at_g(k):
        return lambda i, rows: grads.at[k, i, 0] if rows is None else grads.at[k, i, 0, rows]

    rounds = {k: ring_gather(net, at_g(k), near, far) for k in range(4)}
    rounds[0][0]()
    output[...] = (hidden * sig).astype(BF16)
    last = {}

    def swap(k):
        rounds[k][2]()
        last[k] = net.send(grads.at[k, :, 0], grads.at[k, :, 1], other)

    out_copies[1].wait_recv()
    rounds[1][0]()
    rounds[0][1]()
    out_copies[2].wait_recv()
    rounds[2][0]()
    rounds[1][1]()
    swap(0)
    out_copies[3].wait_recv()
    rounds[3][0]()
    rounds[2][1]()
    swap(1)
    rounds[3][1]()
    swap(2)
    swap(3)
    for k in range(4):
        last[k].wait_recv()
    net.finish()


def final_kernel(
    partial, features, weight, grad_features, grad_weight,
    from_y, total, from_zh, shares, got8, sum8, got4, got16, all4, all8, send_sems, recv_sems,
):
    place = Place()
    net = Net(send_sems, recv_sems)
    y_peers = {i: place.peer(y=i) for i in (1, 2, 3)}
    z_pairs = [(h, l) for h in range(4) for l in range(4) if h or l]
    z_peers = {pair: place.peer(zh=pair[0], zl=pair[1]) for pair in z_pairs}
    x_pairs = [(i, j) for i in range(4) for j in range(2) if i or j]
    x_peers = {pair: place.peer(x=pair[0], core=pair[1]) for pair in x_pairs}
    greet(tuple(y_peers.values()) + tuple(z_peers.values()) + tuple(x_peers.values()))
    order = (2, 1, 3, 0)

    def at_y(k):
        return lambda i, rows: partial.at[i, k, rows]

    rings = {k: ring_scatter(net, at_y(k), from_y.at[k], y_peers[1], y_peers[3]) for k in order}
    z_near, z_far = z_peers[(1, 0)], z_peers[(3, 0)]

    def close(k):
        rings[k][2]()
        total[k] = add(partial[0, k], from_y[k, 0], from_y[k, 1])

    rings[2][0]()
    rings[1][0]()
    rings[2][1]()
    rings[3][0]()
    rings[1][1]()
    close(2)
    transit1 = net.send(total.at[2, LOW], from_zh.at[2, LOW], z_near)
    transit3 = net.send(total.at[2, HIGH], from_zh.at[2, HIGH], z_far)
    rings[0][0]()
    rings[3][1]()
    close(1)
    near0 = net.send(total.at[1, LOW], from_zh.at[0, LOW], z_near)
    rings[0][1]()
    close(3)
    far1 = net.send(total.at[3, HIGH], from_zh.at[1, HIGH], z_far)
    transit1.wait_recv()
    total[3, LOW] = add(total[3, LOW], from_zh[2, LOW])
    far0 = net.send(total.at[3, LOW], from_zh.at[1, LOW], z_far)
    transit3.wait_recv()
    total[1, HIGH] = add(total[1, HIGH], from_zh[2, HIGH])
    near1 = net.send(total.at[1, HIGH], from_zh.at[0, HIGH], z_near)
    rings[0][2]()
    own = partial[0, 0].astype(F32) + from_y[0, 0].astype(F32) + from_y[0, 1].astype(F32)
    for copy in (near0, far1, far0, near1):
        copy.wait_recv()
    own = own + from_zh[0].astype(F32) + from_zh[1].astype(F32)
    projected = own.astype(BF16)

    term = lax.dot_general(
        features[...], projected, (((0,), (0,)), ((), ())), preferred_element_type=F32
    ).astype(BF16)
    for p in range(8):
        for q in range(4):
            rows = p * 32 + (q // 2) * 16
            lanes = (q % 2) * 128
            shares[p, q] = term[rows:rows + 16, lanes:lanes + 128]

    me8 = place.x * 2 + place.core
    me16 = place.zh * 4 + place.zl
    copies = []
    for n, (i, j) in enumerate(x_pairs):
        there = FLIPS[i](place.x) * 2 + FLIPS[j](place.core)
        copies.append(net.send(shares.at[there], got8.at[n], x_peers[(i, j)]))
    grad_features[...] = lax.dot_general(
        projected, weight[...], (((1,), (1,)), ((), ())), preferred_element_type=F32
    ).astype(BF16)
    sum_own = shares[me8].astype(F32)
    for n, copy in enumerate(copies):
        copy.wait_recv()
        sum_own = sum_own + got8[n].astype(F32)
    sum8[...] = sum_own.astype(BF16)

    copies = [
        net.send(sum8.at[FLIPS[i](place.y)], got4.at[i - 1], y_peers[i]) for i in (1, 2, 3)
    ]
    sum_own = sum8[place.y].astype(F32)
    for i, copy in enumerate(copies):
        copy.wait_recv()
        sum_own = sum_own + got4[i].astype(F32)
    got16[me16] = sum_own.astype(BF16)

    copies = [net.send(got16.at[me16], got16.at[me16], z_peers[pair]) for pair in z_pairs]
    for copy in copies:
        copy.wait_recv()
    sum_all = got16[0].astype(F32)
    for n in range(1, 16):
        sum_all = sum_all + got16[n].astype(F32)
    all4[place.y] = sum_all.astype(BF16)

    copies = [net.send(all4.at[place.y], all4.at[place.y], y_peers[i]) for i in (1, 2, 3)]
    for copy in copies:
        copy.wait_recv()
    all8[me8] = all4[...]
    copies = [net.send(all4, all8.at[me8], x_peers[pair]) for pair in x_pairs]
    for copy in copies:
        copy.wait_recv()
    for p in range(8):
        for q in range(4):
            rows = p * 32 + (q // 2) * 16
            lanes = (q % 2) * 128
            grad_weight[rows:rows + 16, lanes:lanes + 128] = all8[p, q].astype(F32)
    net.finish()


VM = pl.BlockSpec(memory_space=pltpu.VMEM)
SM = pl.BlockSpec(memory_space=pltpu.SMEM)
ANY = pl.BlockSpec(memory_space=pl.ANY)


def shape(*dims, dtype=BF16):
    return jax.ShapeDtypeStruct(dims, dtype)


def comm_params(number):
    return pltpu.CompilerParams(
        collective_id=number, has_side_effects=True, vmem_limit_bytes=VMEM_LIMIT
    )


def links(count):
    return [pltpu.SemaphoreType.DMA((count,)), pltpu.SemaphoreType.DMA((count,))]


def products(back, enc, count, tiles, panel):
    targets = TCOLS if back else TROWS
    return pl.pallas_call(
        functools.partial(products_kernel, back),
        out_shape=shape(targets, TILE, HID),
        in_specs=[SM, SM, ANY, VM],
        out_specs=VM,
        scratch_shapes=[
            pltpu.VMEM((SLOTS, TILE, TILE), BF16),
            pltpu.VMEM((targets + 1, TILE, HID), F32),
            pltpu.SemaphoreType.DMA((SLOTS // GROUP,)),
        ],
        compiler_params=pltpu.CompilerParams(vmem_limit_bytes=VMEM_LIMIT),
        name="back_products" if back else "products",
    )(enc, count, tiles, panel)


def body(features, weight, tiles, coords, counts, cotangent):
    my_coords = coords[0, 0]
    enc = (my_coords[:, 0] ^ lax.axis_index("col")) * 16 + (
        my_coords[:, 1] ^ lax.axis_index("row")
    )
    my_tiles = tiles[0, 0]

    panel = pl.pallas_call(
        gather_kernel,
        out_shape=shape(4, 4, TILE, HID),
        in_specs=[VM, VM],
        out_specs=VM,
        scratch_shapes=links(20),
        compiler_params=comm_params(1),
        name="gather_panel",
    )(features, weight)

    partial = products(False, enc, counts, my_tiles, panel.reshape(TCOLS, TILE, HID))

    output, grads = pl.pallas_call(
        middle_kernel,
        out_shape=(shape(TILE, HID), shape(4, 4, 2, TILE, HID)),
        in_specs=[VM, VM],
        out_specs=(VM, VM),
        scratch_shapes=[
            pltpu.VMEM((4, 4, TILE, HID), BF16),
            pltpu.VMEM((4, 3, TILE, HID), BF16),
            pltpu.VMEM((4, TILE, HID), BF16),
            pltpu.VMEM((4, TILE, HID), BF16),
        ] + links(64),
        compiler_params=comm_params(2),
        name="hidden_and_slope",
    )(partial.reshape(4, 4, 2, TILE, HID), cotangent)

    back = products(True, enc, counts, my_tiles, grads.reshape(TROWS, TILE, HID))

    grad_features, grad_weight = pl.pallas_call(
        final_kernel,
        out_shape=(shape(TILE, HID), shape(HID, HID, dtype=F32)),
        in_specs=[VM, VM, VM],
        out_specs=(VM, VM),
        scratch_shapes=[
            pltpu.VMEM((4, 3, TILE, HID), BF16),
            pltpu.VMEM((4, TILE, HID), BF16),
            pltpu.VMEM((3, TILE, HID), BF16),
            pltpu.VMEM((8, 4, 16, 128), BF16),
            pltpu.VMEM((7, 4, 16, 128), BF16),
            pltpu.VMEM((4, 16, 128), BF16),
            pltpu.VMEM((3, 16, 128), BF16),
            pltpu.VMEM((16, 16, 128), BF16),
            pltpu.VMEM((4, 16, 128), BF16),
            pltpu.VMEM((8, 4, 16, 128), BF16),
        ] + links(68),
        compiler_params=comm_params(3),
        name="gradients",
    )(back.reshape(4, 4, TILE, HID), features, weight)
    return output, grad_features, grad_weight


def solution(mesh):
    placed = (
        P(("col", "row"), None),
        P(),
        P("row", "col", None, None, None),
        P("row", "col", None, None),
        P("row", "col"),
        P(("row", "col"), None),
    )
    return jax.shard_map(
        body,
        mesh=mesh,
        in_specs=placed,
        out_specs=(P(("row", "col"), None), P(("col", "row"), None), P()),
        check_vma=False,
    )
```

```python
import jax
import jax.numpy as jnp
from jax import lax
from jax.experimental import pallas as pl
from jax.experimental.pallas import tpu as pltpu
from jax.sharding import PartitionSpec as P

F32 = jnp.float32
BF16 = jnp.bfloat16
MESH = pl.DeviceIdType.MESH
TILE = 128
HID = 256
TROWS = 32
TCOLS = 16
SLOTS = 96
VMEM_LIMIT = 58 * 2**20


def flip1(v):
    return v + 1 - 2 * lax.rem(v, 2)


def flip2(v):
    return lax.rem(v + 2, 4)


def flip3(v):
    return 3 - v


FLIPS = {0: lambda v: v, 1: flip1, 2: flip2, 3: flip3}


class Place:
    def __init__(self):
        row = lax.axis_index("row")
        col = lax.axis_index("col")
        self.y = lax.div(row, 4)
        self.zh = lax.rem(row, 4)
        self.zl = lax.div(col, 8)
        self.x = lax.rem(lax.div(col, 2), 4)
        self.core = lax.rem(col, 2)

    def peer(self, y=0, zh=0, zl=0, x=0, core=0):
        row = FLIPS[y](self.y) * 4 + FLIPS[zh](self.zh)
        col = FLIPS[zl](self.zl) * 8 + FLIPS[x](self.x) * 2 + FLIPS[core](self.core)
        return (row, col)


class Net:
    def __init__(self, send_sems, recv_sems):
        self.send_sems = send_sems
        self.recv_sems = recv_sems
        self.started = []

    def send(self, src, dst, device):
        i = len(self.started)
        copy = pltpu.make_async_remote_copy(
            src_ref=src,
            dst_ref=dst,
            send_sem=self.send_sems.at[i],
            recv_sem=self.recv_sems.at[i],
            device_id=device,
            device_id_type=MESH,
        )
        copy.start()
        self.started.append(copy)
        return copy

    def finish(self):
        for copy in self.started:
            copy.wait_send()


def greet(peers):
    barrier = pltpu.get_barrier_semaphore()
    for peer in peers:
        pl.semaphore_signal(barrier, inc=1, device_id=peer, device_id_type=MESH)
    pl.semaphore_wait(barrier, len(peers))


def add(*values):
    total = values[0].astype(F32)
    for value in values[1:]:
        total = total + value.astype(F32)
    return total.astype(BF16)


def ring_gather(net, at, near, far):
    copies = {}

    def first():
        copies["n0"] = net.send(at(0, 0), at(1, 0), near)
        copies["f1"] = net.send(at(0, 1), at(3, 1), far)
        copies["n1"] = net.send(at(0, 1), at(1, 1), near)
        copies["f0"] = net.send(at(0, 0), at(3, 0), far)

    def second():
        copies["n0"].wait_recv()
        copies["nf"] = net.send(at(1, 0), at(2, 0), far)
        copies["f1"].wait_recv()
        copies["fn"] = net.send(at(3, 1), at(2, 1), near)
        copies["n1"].wait_recv()
        copies["f0"].wait_recv()

    def third():
        copies["nf"].wait_recv()
        copies["fn"].wait_recv()

    return first, second, third


def ring_scatter(net, at, landing, near, far):
    copies = {}

    def first():
        copies["t1"] = net.send(at(2, 0), landing(2, 0), near)
        copies["t3"] = net.send(at(2, 1), landing(2, 1), far)
        copies["n0"] = net.send(at(1, 0), landing(0, 0), near)
        copies["f1"] = net.send(at(3, 1), landing(1, 1), far)

    def second():
        copies["t1"].wait_recv()
        share = at(3, 0)
        share[...] = add(share[...], landing(2, 0)[...])
        copies["f0"] = net.send(share, landing(1, 0), far)
        copies["t3"].wait_recv()
        share = at(1, 1)
        share[...] = add(share[...], landing(2, 1)[...])
        copies["n1"] = net.send(share, landing(0, 1), near)

    def third():
        for name in ("n0", "f1", "f0", "n1"):
            copies[name].wait_recv()

    return first, second, third


def halves(size):
    half = size // 2
    return {0: slice(0, half), 1: slice(half, size), None: slice(None)}


def kernel(
    slots, features, weight, tiles, cotangent,
    output, grad_features, grad_weight,
    held, feats, panel, mat, acc, partial, from_core, from_x, total_x, from_z,
    grads, back_acc, back, from_y, total_y, from_zh,
    cot, shares, got8, sum8, got4, got16, all4, all8,
    local_sems, send_sems, recv_sems,
):
    place = Place()
    net = Net(send_sems, recv_sems)
    node = halves(TILE)
    wide = halves(HID)

    load_feats = pltpu.make_async_copy(features, feats.at[0, 0], local_sems.at[0])
    load_weight = pltpu.make_async_copy(weight, mat, local_sems.at[1])
    load_tiles = pltpu.make_async_copy(tiles, held.at[pl.ds(0, SLOTS)], local_sems.at[2])
    load_cot = pltpu.make_async_copy(cotangent, cot, local_sems.at[3])
    for copy in (load_feats, load_weight, load_tiles, load_cot):
        copy.start()

    y_peers = {i: place.peer(y=i) for i in (1, 2, 3)}
    z_pairs = [(h, l) for h in range(4) for l in range(4) if h or l]
    z_peers = {pair: place.peer(zh=pair[0], zl=pair[1]) for pair in z_pairs}
    x_pairs = [(i, j) for i in range(4) for j in range(2) if i or j]
    x_peers = {pair: place.peer(x=pair[0], core=pair[1]) for pair in x_pairs}
    greet(tuple(y_peers.values()) + tuple(z_peers.values()) + tuple(x_peers.values()))
    zh_near, zh_far = z_peers[(1, 0)], z_peers[(3, 0)]
    y_near, y_far = y_peers[1], y_peers[3]
    x_near, x_far = x_peers[(1, 0)], x_peers[(3, 0)]
    other = x_peers[(0, 1)]
    along = {k: z_peers[(0, k)] for k in (1, 2, 3)}

    def at_zh(i, half):
        return feats.at[0, i, node[half]]

    def at_y(k):
        return lambda i, half: feats.at[i, k, node[half]]

    load_feats.wait()
    z_ring = ring_gather(net, at_zh, zh_near, zh_far)
    rings = {k: ring_gather(net, at_y(k), y_near, y_far) for k in (0, 1, 3)}
    z_ring[0]()
    rings[0][0]()
    held[SLOTS] = jnp.zeros((TILE, TILE), BF16)
    load_weight.wait()

    def project(k):
        def one(i, carry):
            panel[i, k] = jnp.dot(
                feats[i, k], mat[...], preferred_element_type=F32
            ).astype(BF16)
            return carry

        lax.fori_loop(0, 4, one, 0)

    def forward(targets, ks):
        places = [(i, k) for k in ks for i in range(4)]
        left = jnp.concatenate(
            [
                jnp.concatenate([held[slots[t * TCOLS + i * 4 + k]] for i, k in places], axis=1)
                for t in targets
            ],
            axis=0,
        )
        right = jnp.concatenate([panel[i, k] for i, k in places], axis=0)
        return jnp.dot(left, right, preferred_element_type=F32)

    def sweep(ks, first):
        def block(b, carry):
            targets = [b * 4 + i for i in range(4)]
            value = forward(targets, ks).reshape(4, TILE, HID)
            rows = pl.ds(b * 4, 4)
            acc[rows] = value if first else acc[rows] + value
            return carry

        lax.fori_loop(0, TROWS // 4, block, 0)

    rings[0][1]()
    z_ring[1]()
    rings[1][0]()
    rings[3][0]()
    rings[0][2]()
    load_tiles.wait()
    project(0)
    rings[1][1]()
    rings[3][1]()
    sweep((0,), True)
    z_ring[2]()
    direct = [net.send(feats.at[0, 2], feats.at[i, 2], y_peers[i]) for i in (1, 3, 2)]
    rings[1][2]()
    rings[3][2]()
    project(1)
    project(3)
    sweep((1, 3), False)
    for copy in direct:
        copy.wait_recv()
    project(2)

    order = (3, 2, 1, 0)

    def finish_block(k, core):
        targets = [k * 8 + x * 2 + core for x in range(4)]
        value = forward(targets, (2,))
        for x, t in enumerate(targets):
            rows = slice(x * TILE, (x + 1) * TILE)
            partial[k, x, core] = (acc[t] + value[rows]).astype(BF16)

    core_copies = {}
    for k in order:
        finish_block(k, 1)
        core_copies[k] = net.send(partial.at[k, :, 1], from_core.at[k], other)

    def at_x(k):
        return lambda i, half: from_core.at[k, i, node[half]]

    def land_x(k):
        return lambda i, half: from_x.at[k, i, node[half]]

    rings = {k: ring_scatter(net, at_x(k), land_x(k), x_near, x_far) for k in order}
    z_copies = {}

    def start(k):
        finish_block(k, 0)
        core_copies[k].wait_recv()
        for i in (2, 1, 3):
            from_core[k, i] = add(from_core[k, i], partial[k, i, 0])
        rings[k][0]()

    def close(k):
        rings[k][2]()
        parts = (partial[k, 0, 0], from_core[k, 0], from_x[k, 0], from_x[k, 1])
        if k:
            total_x[k] = add(*parts)
            z_copies[k] = net.send(total_x.at[k], from_z.at[k], along[k])
            return None
        return sum(part.astype(F32) for part in parts)

    start(3)
    start(2)
    start(1)
    rings[3][1]()
    start(0)
    rings[2][1]()
    close(3)
    rings[1][1]()
    close(2)
    rings[0][1]()
    close(1)
    hidden = close(0)
    load_cot.wait()
    for k in (3, 2, 1):
        z_copies[k].wait_recv()
        hidden = hidden + from_z[k].astype(F32)
    sig = jax.nn.sigmoid(hidden)
    slope = sig * (1.0 + hidden * (1.0 - sig))
    grads[0, 0, 0] = (cot[...].astype(F32) * slope).T.astype(BF16)

    out_copies = {k: net.send(grads.at[0, 0, 0], grads.at[k, 0, 0], along[k]) for k in (1, 2, 3)}

    def at_g(k):
        return lambda i, half: grads.at[k, i, 0, wide[half]]

    rounds = {k: ring_gather(net, at_g(k), x_near, x_far) for k in range(4)}
    rounds[0][0]()
    output[...] = (hidden * sig).astype(BF16)
    last = {}

    def swap(k):
        rounds[k][2]()
        last[k] = net.send(grads.at[k, :, 0], grads.at[k, :, 1], other)

    def backward(k, p):
        left = jnp.concatenate([grads[k, x, c] for x in range(4) for c in range(2)], axis=1)
        right = jnp.concatenate(
            [
                jnp.concatenate(
                    [held[slots[(k * 8 + j) * TCOLS + 2 * p + i]] for i in range(2)], axis=1
                )
                for j in range(8)
            ],
            axis=0,
        )
        return jnp.dot(left, right, preferred_element_type=F32)

    def back_sweep(k, first):
        last[k].wait_recv()

        def block(p, carry):
            value = backward(k, p)
            back_acc[p] = value if first else back_acc[p] + value
            return carry

        lax.fori_loop(0, TCOLS // 2, block, 0)

    out_copies[1].wait_recv()
    rounds[1][0]()
    rounds[0][1]()
    out_copies[2].wait_recv()
    rounds[2][0]()
    rounds[1][1]()
    swap(0)
    out_copies[3].wait_recv()
    rounds[3][0]()
    rounds[2][1]()
    swap(1)
    back_sweep(0, True)
    rounds[3][1]()
    swap(2)
    back_sweep(1, False)
    swap(3)
    back_sweep(2, False)
    last[3].wait_recv()

    def at_b(k):
        return lambda i, half: back.at[i, k, wide[half]]

    def land_y(k):
        return lambda i, half: from_y.at[k, i, wide[half]]

    rings = {k: ring_scatter(net, at_b(k), land_y(k), y_near, y_far) for k in range(4)}

    def back_pairs(pair):
        def block(i, carry):
            p = i * 2 + pair
            value = (back_acc[p] + backward(3, p)).astype(BF16)
            back[i, 2 * pair] = value[:, :TILE]
            back[i, 2 * pair + 1] = value[:, TILE:]
            return carry

        lax.fori_loop(0, 4, block, 0)

    back_pairs(1)
    rings[2][0]()
    rings[3][0]()
    back_pairs(0)
    rings[1][0]()

    chunks = [(i, k) for i in range(4) for k in range(4)]
    term = jnp.dot(
        jnp.concatenate([back[i, k] for i, k in chunks], axis=1),
        jnp.concatenate([feats[i, k] for i, k in chunks], axis=0),
        preferred_element_type=F32,
    ).astype(BF16)
    rings[0][0]()
    for p in range(8):
        for q in range(4):
            rows = p * 32 + (q // 2) * 16
            lanes = (q % 2) * 128
            shares[p, q] = term[rows:rows + 16, lanes:lanes + 128]
    me8 = place.x * 2 + place.core
    me16 = place.zh * 4 + place.zl
    copies8 = []
    for n, (i, j) in enumerate(x_pairs):
        there = FLIPS[i](place.x) * 2 + FLIPS[j](place.core)
        copies8.append(net.send(shares.at[there], got8.at[n], x_peers[(i, j)]))

    def close_y(k):
        rings[k][2]()
        total_y[k] = add(back[0, k], from_y[k, 0], from_y[k, 1])

    def zh_send(k, slot, half, peer):
        return net.send(total_y.at[k, wide[half]], from_zh.at[slot, wide[half]], peer)

    rings[2][1]()
    rings[3][1]()
    rings[1][1]()
    close_y(2)
    transit1 = zh_send(2, 2, 0, zh_near)
    transit3 = zh_send(2, 2, 1, zh_far)

    sum_own = shares[me8].astype(F32)
    for n, copy in enumerate(copies8):
        copy.wait_recv()
        sum_own = sum_own + got8[n].astype(F32)
    sum8[...] = sum_own.astype(BF16)
    copies4 = [
        net.send(sum8.at[FLIPS[i](place.y)], got4.at[i - 1], y_peers[i]) for i in (1, 2, 3)
    ]

    close_y(3)
    far1 = zh_send(3, 1, 1, zh_far)
    close_y(1)
    near0 = zh_send(1, 0, 0, zh_near)
    rings[0][1]()

    sum_own = sum8[place.y].astype(F32)
    for i, copy in enumerate(copies4):
        copy.wait_recv()
        sum_own = sum_own + got4[i].astype(F32)
    got16[me16] = sum_own.astype(BF16)
    copies16 = [net.send(got16.at[me16], got16.at[me16], z_peers[pair]) for pair in z_pairs]

    transit1.wait_recv()
    total_y[3, wide[0]] = add(total_y[3, wide[0]], from_zh[2, wide[0]])
    far0 = zh_send(3, 1, 0, zh_far)
    transit3.wait_recv()
    total_y[1, wide[1]] = add(total_y[1, wide[1]], from_zh[2, wide[1]])
    near1 = zh_send(1, 0, 1, zh_near)
    rings[0][2]()
    own = back[0, 0].astype(F32) + from_y[0, 0].astype(F32) + from_y[0, 1].astype(F32)

    for copy in copies16:
        copy.wait_recv()
    sum_all = got16[0].astype(F32)
    for n in range(1, 16):
        sum_all = sum_all + got16[n].astype(F32)
    all4[place.y] = sum_all.astype(BF16)
    copies4 = [net.send(all4.at[place.y], all4.at[place.y], y_peers[i]) for i in (1, 2, 3)]

    for copy in (near0, far1, far0, near1):
        copy.wait_recv()
    own = own + from_zh[0].astype(F32) + from_zh[1].astype(F32)
    grad_features[...] = lax.dot_general(
        own.T.astype(BF16), mat[...], (((1,), (1,)), ((), ())), preferred_element_type=F32
    ).astype(BF16)

    for copy in copies4:
        copy.wait_recv()
    copies8 = [net.send(all4, all8.at[me8], x_peers[pair]) for pair in x_pairs]
    all8[me8] = all4[...]
    for copy in copies8:
        copy.wait_recv()
    for p in range(8):
        for q in range(4):
            rows = p * 32 + (q // 2) * 16
            lanes = (q % 2) * 128
            grad_weight[rows:rows + 16, lanes:lanes + 128] = all8[p, q].astype(F32)
    net.finish()


VM = pl.BlockSpec(memory_space=pltpu.VMEM)
SM = pl.BlockSpec(memory_space=pltpu.SMEM)
ANY = pl.BlockSpec(memory_space=pl.ANY)
LINKS = 160


def shape(*dims, dtype=BF16):
    return jax.ShapeDtypeStruct(dims, dtype)


def buf(*dims, dtype=BF16):
    return pltpu.VMEM(dims, dtype)


def body(features, weight, tiles, coords, counts, cotangent):
    my_coords = coords[0, 0]
    code = (my_coords[:, 0] ^ lax.axis_index("col")) * TCOLS + (
        my_coords[:, 1] ^ lax.axis_index("row")
    )
    slot = jnp.arange(SLOTS, dtype=jnp.int32)
    code = jnp.where(slot < counts[0, 0], code, -1)
    place = jnp.arange(TROWS * TCOLS, dtype=jnp.int32)
    hit = code[:, None] == place[None, :]
    slots = SLOTS + jnp.sum(jnp.where(hit, slot[:, None] - SLOTS, 0), axis=0, dtype=jnp.int32)

    output, grad_features, grad_weight = pl.pallas_call(
        kernel,
        out_shape=(shape(TILE, HID), shape(TILE, HID), shape(HID, HID, dtype=F32)),
        in_specs=[SM, ANY, ANY, ANY, ANY],
        out_specs=(VM, VM, VM),
        scratch_shapes=[
            buf(SLOTS + 1, TILE, TILE),
            buf(4, 4, TILE, HID),
            buf(4, 4, TILE, HID),
            buf(HID, HID),
            buf(TROWS, TILE, HID, dtype=F32),
            buf(4, 4, 2, TILE, HID),
            buf(4, 4, TILE, HID),
            buf(4, 3, TILE, HID),
            buf(4, TILE, HID),
            buf(4, TILE, HID),
            buf(4, 4, 2, HID, TILE),
            buf(TCOLS // 2, HID, HID, dtype=F32),
            buf(4, 4, HID, TILE),
            buf(4, 3, HID, TILE),
            buf(4, HID, TILE),
            buf(3, HID, TILE),
            buf(TILE, HID),
            buf(8, 4, 16, 128),
            buf(7, 4, 16, 128),
            buf(4, 16, 128),
            buf(3, 16, 128),
            buf(16, 16, 128),
            buf(4, 16, 128),
            buf(8, 4, 16, 128),
            pltpu.SemaphoreType.DMA((4,)),
            pltpu.SemaphoreType.DMA((LINKS,)),
            pltpu.SemaphoreType.DMA((LINKS,)),
        ],
        compiler_params=pltpu.CompilerParams(
            collective_id=1, has_side_effects=True, vmem_limit_bytes=VMEM_LIMIT
        ),
        name="layer",
    )(slots, features, weight, tiles[0, 0], cotangent)
    return output, grad_features, grad_weight.T


def solution(mesh):
    placed = (
        P(("col", "row"), None),
        P(),
        P("row", "col", None, None, None),
        P("row", "col", None, None),
        P("row", "col"),
        P(("row", "col"), None),
    )
    return jax.shard_map(
        body,
        mesh=mesh,
        in_specs=placed,
        out_specs=(P(("row", "col"), None), P(("col", "row"), None), P()),
        check_vma=False,
    )
```

```python
import jax
import jax.numpy as jnp
from jax import lax
from jax.experimental import pallas as pl
from jax.experimental.pallas import tpu as pltpu
from jax.sharding import PartitionSpec as P

F32 = jnp.float32
BF16 = jnp.bfloat16
MESH = pl.DeviceIdType.MESH
TILE = 128
HID = 256
TROWS = 32
TCOLS = 16
SLOTS = 96
VMEM_LIMIT = 58 * 2**20


def flip1(v):
    return v + 1 - 2 * lax.rem(v, 2)


def flip2(v):
    return lax.rem(v + 2, 4)


def flip3(v):
    return 3 - v


FLIPS = {0: lambda v: v, 1: flip1, 2: flip2, 3: flip3}


class Place:
    def __init__(self):
        row = lax.axis_index("row")
        col = lax.axis_index("col")
        self.y = lax.div(row, 4)
        self.zh = lax.rem(row, 4)
        self.zl = lax.div(col, 8)
        self.x = lax.rem(lax.div(col, 2), 4)
        self.core = lax.rem(col, 2)

    def peer(self, y=0, zh=0, zl=0, x=0, core=0):
        row = FLIPS[y](self.y) * 4 + FLIPS[zh](self.zh)
        col = FLIPS[zl](self.zl) * 8 + FLIPS[x](self.x) * 2 + FLIPS[core](self.core)
        return (row, col)


class Net:
    def __init__(self, send_sems, recv_sems):
        self.send_sems = send_sems
        self.recv_sems = recv_sems
        self.started = []

    def send(self, src, dst, device):
        i = len(self.started)
        copy = pltpu.make_async_remote_copy(
            src_ref=src,
            dst_ref=dst,
            send_sem=self.send_sems.at[i],
            recv_sem=self.recv_sems.at[i],
            device_id=device,
            device_id_type=MESH,
        )
        copy.start()
        self.started.append(copy)
        return copy

    def finish(self):
        for copy in self.started:
            copy.wait_send()


def greet(peers):
    barrier = pltpu.get_barrier_semaphore()
    for peer in peers:
        pl.semaphore_signal(barrier, inc=1, device_id=peer, device_id_type=MESH)
    return lambda: pl.semaphore_wait(barrier, len(peers))


def add(*values):
    total = values[0].astype(F32)
    for value in values[1:]:
        total = total + value.astype(F32)
    return total.astype(BF16)


def ring_gather(net, at, near, far):
    copies = {}

    def first():
        copies["n0"] = net.send(at(0, 0), at(1, 0), near)
        copies["f1"] = net.send(at(0, 1), at(3, 1), far)
        copies["n1"] = net.send(at(0, 1), at(1, 1), near)
        copies["f0"] = net.send(at(0, 0), at(3, 0), far)

    def second():
        copies["n0"].wait_recv()
        copies["nf"] = net.send(at(1, 0), at(2, 0), far)
        copies["f1"].wait_recv()
        copies["fn"] = net.send(at(3, 1), at(2, 1), near)
        copies["n1"].wait_recv()
        copies["f0"].wait_recv()

    def third():
        copies["nf"].wait_recv()
        copies["fn"].wait_recv()

    third.halves = (lambda: copies["nf"].wait_recv(), lambda: copies["fn"].wait_recv())
    return first, second, third


def ring_scatter(net, at, landing, near, far):
    copies = {}

    def first():
        copies["t1"] = net.send(at(2, 0), landing(2, 0), near)
        copies["t3"] = net.send(at(2, 1), landing(2, 1), far)
        copies["n0"] = net.send(at(1, 0), landing(0, 0), near)
        copies["f1"] = net.send(at(3, 1), landing(1, 1), far)

    def second():
        copies["t1"].wait_recv()
        share = at(3, 0)
        share[...] = add(share[...], landing(2, 0)[...])
        copies["f0"] = net.send(share, landing(1, 0), far)
        copies["t3"].wait_recv()
        share = at(1, 1)
        share[...] = add(share[...], landing(2, 1)[...])
        copies["n1"] = net.send(share, landing(0, 1), near)

    def third():
        for name in ("n0", "f1", "f0", "n1"):
            copies[name].wait_recv()

    return first, second, third


def halves(size):
    half = size // 2
    return {0: slice(0, half), 1: slice(half, size), None: slice(None)}


def kernel(
    coords, count, features, weight, tiles, cotangent,
    output, grad_features, grad_weight,
    held, feats, mat, acc, partial, from_core, from_x, total_x, from_z,
    grads, back_acc, back, from_y, direct_y, total_y, from_zh,
    cot, shares, got8, sum8, got4, got16, all4, all8, spots, places, slots,
    local_sems, send_sems, recv_sems,
):
    place = Place()
    net = Net(send_sems, recv_sems)
    node = halves(TILE)
    wide = halves(HID)

    y_peers = {i: place.peer(y=i) for i in (1, 2, 3)}
    z_pairs = [(h, l) for h in range(4) for l in range(4) if h or l]
    z_peers = {pair: place.peer(zh=pair[0], zl=pair[1]) for pair in z_pairs}
    x_pairs = [(i, j) for i in range(4) for j in range(2) if i or j]
    x_peers = {pair: place.peer(x=pair[0], core=pair[1]) for pair in x_pairs}
    arrived = greet(tuple(y_peers.values()) + tuple(z_peers.values()) + tuple(x_peers.values()))
    load_feats = pltpu.make_async_copy(features, feats.at[0, 0], local_sems.at[0])
    load_weight = pltpu.make_async_copy(weight, mat, local_sems.at[1])
    load_tiles = pltpu.make_async_copy(tiles, held.at[pl.ds(0, SLOTS)], local_sems.at[2])
    load_cot = pltpu.make_async_copy(cotangent, cot, local_sems.at[3])
    for copy in (load_feats, load_tiles, load_weight, load_cot):
        copy.start()

    zh_near, zh_far = z_peers[(1, 0)], z_peers[(3, 0)]
    y_near, y_far = y_peers[1], y_peers[3]
    x_near, x_far = x_peers[(1, 0)], x_peers[(3, 0)]
    other = x_peers[(0, 1)]
    along = {k: z_peers[(0, k)] for k in (1, 2, 3)}

    def at_zh(i, half):
        return feats.at[0, i, node[half]]

    def at_y(k):
        return lambda i, half: feats.at[i, k, node[half]]

    load_feats.wait()
    arrived()
    z_ring = ring_gather(net, at_zh, zh_near, zh_far)
    rings = {k: ring_gather(net, at_y(k), y_near, y_far) for k in (0, 1, 3)}
    z_ring[0]()
    rings[0][0]()

    spots[...] = jnp.zeros((8, 128), jnp.int32)
    spots[0:2, 0:SLOTS] = coords[...]
    far_row = jnp.broadcast_to(spots[0:1, :], (128, 128)).T[:SLOTS] ^ lax.axis_index("col")
    far_col = jnp.broadcast_to(spots[1:2, :], (128, 128)).T[:SLOTS] ^ lax.axis_index("row")
    slot = lax.broadcasted_iota(jnp.int32, (SLOTS, 128), 0)
    lane = lax.broadcasted_iota(jnp.int32, (SLOTS, 128), 1)
    value = jnp.where((far_col == lane) & (slot < count[0, 0]), slot - SLOTS, 0)
    for t in range(TROWS):
        found = jnp.where(far_row == t, value, 0)
        places[t:t + 1] = SLOTS + jnp.sum(found, axis=0, keepdims=True)
    load_slots = pltpu.make_async_copy(places, slots, local_sems.at[4])
    load_slots.start()
    held[SLOTS] = jnp.zeros((TILE, TILE), BF16)

    def forward(targets, ks):
        places = [(i, k) for k in ks for i in range(4)]
        left = jnp.concatenate(
            [
                jnp.concatenate([held[slots[t, i * 4 + k]] for i, k in places], axis=1)
                for t in targets
            ],
            axis=0,
        )
        right = jnp.concatenate([feats[i, k] for i, k in places], axis=0)
        return jnp.dot(left, right, preferred_element_type=F32)

    def sweep(ks, first):
        def block(b, carry):
            targets = [b * 4 + i for i in range(4)]
            value = forward(targets, ks).reshape(4, TILE, HID)
            rows = pl.ds(b * 4, 4)
            acc[rows] = value if first else acc[rows] + value
            return carry

        lax.fori_loop(0, TROWS // 4, block, 0)

    z_ring[1]()
    rings[1][0]()
    rings[3][0]()
    rings[0][1]()
    rings[0][2]()
    load_tiles.wait()
    load_slots.wait()
    sweep((0,), True)
    rings[1][1]()
    rings[3][1]()
    direct = []
    for wait, half in zip(z_ring[2].halves, (0, 1)):
        wait()
        for i in (2, 1, 3):
            direct.append(net.send(at_zh(2, half), at_y(2)(i, half), y_peers[i]))
    rings[1][2]()
    rings[3][2]()
    sweep((1, 3), False)
    for copy in direct:
        copy.wait_recv()

    order = (3, 2, 1, 0)

    def finish_block(k, core):
        targets = [k * 8 + x * 2 + core for x in range(4)]
        value = forward(targets, (2,))
        for x, t in enumerate(targets):
            rows = slice(x * TILE, (x + 1) * TILE)
            partial[k, x, core] = (acc[t] + value[rows]).astype(BF16)

    core_copies = {}
    for k in order:
        finish_block(k, 1)
        core_copies[k] = net.send(partial.at[k, :, 1], from_core.at[k], other)

    def at_x(k):
        return lambda i, half: from_core.at[k, i, node[half]]

    def land_x(k):
        return lambda i, half: from_x.at[k, i, node[half]]

    rings = {k: ring_scatter(net, at_x(k), land_x(k), x_near, x_far) for k in order}
    z_copies = {}

    def start(k):
        finish_block(k, 0)
        core_copies[k].wait_recv()
        for i in (2, 1, 3):
            from_core[k, i] = add(from_core[k, i], partial[k, i, 0])
        rings[k][0]()

    def close(k):
        rings[k][2]()
        parts = (partial[k, 0, 0], from_core[k, 0], from_x[k, 0], from_x[k, 1])
        if k:
            total_x[k] = add(*parts)
            z_copies[k] = net.send(total_x.at[k], from_z.at[k], along[k])
            return None
        return sum(part.astype(F32) for part in parts)

    start(3)
    start(2)
    start(1)
    rings[3][1]()
    start(0)
    rings[2][1]()
    close(3)
    rings[1][1]()
    close(2)
    rings[0][1]()
    close(1)
    own = close(0)
    load_cot.wait()
    load_weight.wait()
    for k in (3, 2, 1):
        z_copies[k].wait_recv()
        own = own + from_z[k].astype(F32)
    summed = own.astype(BF16)
    hidden = jnp.dot(summed, mat[...], preferred_element_type=F32)
    sig = jax.nn.sigmoid(hidden)
    slope = sig * (1.0 + hidden * (1.0 - sig))
    grads[0, 0, 0] = (cot[...].astype(F32) * slope).T.astype(BF16)

    out_copies = {k: net.send(grads.at[0, 0, 0], grads.at[k, 0, 0], along[k]) for k in (1, 2, 3)}

    def at_g(k):
        return lambda i, half: grads.at[k, i, 0, wide[half]]

    rounds = {k: ring_gather(net, at_g(k), x_near, x_far) for k in range(4)}
    rounds[0][0]()
    last = {}

    def unpacked(p, q):
        rows = p * 32 + (q // 2) * 16
        lanes = (q % 2) * 128
        return slice(rows, rows + 16), slice(lanes, lanes + 128)

    me8 = place.x * 2 + place.core
    me16 = place.zh * 4 + place.zl
    sums = {}

    def sum_start():
        term = jnp.dot(grads[0, 0, 0], summed, preferred_element_type=F32).astype(BF16)
        for p in range(8):
            for q in range(4):
                rows, lanes = unpacked(p, q)
                shares[p, q] = term[rows, lanes]
        sums[0] = [
            net.send(
                shares.at[FLIPS[i](place.x) * 2 + FLIPS[j](place.core)],
                got8.at[n], x_peers[(i, j)],
            )
            for n, (i, j) in enumerate(x_pairs)
        ]

    def sum_8():
        total = shares[me8].astype(F32)
        for n, copy in enumerate(sums[0]):
            copy.wait_recv()
            total = total + got8[n].astype(F32)
        sum8[...] = total.astype(BF16)
        sums[1] = [
            net.send(sum8.at[FLIPS[i](place.y)], got4.at[i - 1], y_peers[i]) for i in (1, 2, 3)
        ]

    def sum_4():
        total = sum8[place.y].astype(F32)
        for i, copy in enumerate(sums[1]):
            copy.wait_recv()
            total = total + got4[i].astype(F32)
        got16[me16] = total.astype(BF16)
        sums[2] = [net.send(got16.at[me16], got16.at[me16], z_peers[pair]) for pair in z_pairs]

    def sum_16():
        for copy in sums[2]:
            copy.wait_recv()
        total = got16[0].astype(F32)
        for n in range(1, 16):
            total = total + got16[n].astype(F32)
        all4[place.y] = total.astype(BF16)
        sums[3] = [net.send(all4.at[place.y], all4.at[place.y], y_peers[i]) for i in (1, 2, 3)]

    def spread_4():
        for copy in sums[3]:
            copy.wait_recv()
        sums[4] = [net.send(all4, all8.at[me8], x_peers[pair]) for pair in x_pairs]
        all8[me8] = all4[...]

    def sum_end():
        for copy in sums[4]:
            copy.wait_recv()
        rows = [
            jnp.concatenate([all8[p, q].astype(F32), all8[p, q + 1].astype(F32)], axis=1)
            for p in range(8) for q in (0, 2)
        ]
        grad_weight[...] = jnp.concatenate(rows, axis=0).T

    def swap(k):
        rounds[k][2]()
        last[k] = net.send(grads.at[k, :, 0], grads.at[k, :, 1], other)

    def backward(k, p):
        left = jnp.concatenate([grads[k, x, c] for x in range(4) for c in range(2)], axis=1)
        right = jnp.concatenate(
            [
                jnp.concatenate(
                    [held[slots[k * 8 + j, 2 * p + i]] for i in range(2)], axis=1
                )
                for j in range(8)
            ],
            axis=0,
        )
        return jnp.dot(left, right, preferred_element_type=F32)

    def back_sweep(k, first):
        last[k].wait_recv()

        def block(p, carry):
            value = backward(k, p)
            back_acc[p] = value if first else back_acc[p] + value
            return carry

        lax.fori_loop(0, TCOLS // 2, block, 0)

    sum_start()
    out_copies[1].wait_recv()
    rounds[1][0]()
    rounds[0][1]()
    output[...] = (hidden * sig).astype(BF16)
    out_copies[2].wait_recv()
    rounds[2][0]()
    sum_8()
    rounds[1][1]()
    swap(0)
    out_copies[3].wait_recv()
    rounds[3][0]()
    rounds[2][1]()
    swap(1)
    sum_4()
    back_sweep(0, True)
    rounds[3][1]()
    swap(2)
    back_sweep(1, False)
    swap(3)
    back_sweep(2, False)
    last[3].wait_recv()

    def at_b(k):
        return lambda i, half: back.at[i, k, wide[half]]

    def land_y(k):
        return lambda i, half: from_y.at[k, i, wide[half]]

    rings = {k: ring_scatter(net, at_b(k), land_y(k), y_near, y_far) for k in (0, 1, 3)}

    def back_pairs(pair):
        def block(i, carry):
            p = i * 2 + pair
            value = (back_acc[p] + backward(3, p)).astype(BF16)
            back[i, 2 * pair] = value[:, :TILE]
            back[i, 2 * pair + 1] = value[:, TILE:]
            return carry

        lax.fori_loop(0, 4, block, 0)

    def zh_send(k, slot, half, peer):
        return net.send(total_y.at[k, wide[half]], from_zh.at[slot, wide[half]], peer)

    def close_y(k):
        rings[k][2]()
        total_y[k] = add(back[0, k], from_y[k, 0], from_y[k, 1])

    back_pairs(1)
    direct = {
        half: [net.send(at_b(2)(i, half), direct_y.at[i - 1, wide[half]], y_peers[i]) for i in (2, 1, 3)]
        for half in (0, 1)
    }
    rings[3][0]()
    back_pairs(0)
    rings[1][0]()
    rings[0][0]()
    sum_16()
    transit = {}
    for half, peer in ((0, zh_near), (1, zh_far)):
        for copy in direct[half]:
            copy.wait_recv()
        rows = wide[half]
        total_y[2, rows] = add(
            back[0, 2, rows], direct_y[0, rows], direct_y[1, rows], direct_y[2, rows]
        )
        transit[half] = zh_send(2, 2, half, peer)
    rings[3][1]()
    rings[1][1]()
    rings[0][1]()
    close_y(3)
    far1 = zh_send(3, 1, 1, zh_far)
    close_y(1)
    near0 = zh_send(1, 0, 0, zh_near)
    spread_4()
    transit[0].wait_recv()
    total_y[3, wide[0]] = add(total_y[3, wide[0]], from_zh[2, wide[0]])
    far0 = zh_send(3, 1, 0, zh_far)
    transit[1].wait_recv()
    total_y[1, wide[1]] = add(total_y[1, wide[1]], from_zh[2, wide[1]])
    near1 = zh_send(1, 0, 1, zh_near)
    rings[0][2]()
    own = back[0, 0].astype(F32) + from_y[0, 0].astype(F32) + from_y[0, 1].astype(F32)
    sum_end()
    for copy in (near0, far1, far0, near1):
        copy.wait_recv()
    own = own + from_zh[0].astype(F32) + from_zh[1].astype(F32)
    grad_features[...] = lax.dot_general(
        own.T.astype(BF16), mat[...], (((1,), (1,)), ((), ())), preferred_element_type=F32
    ).astype(BF16)
    net.finish()


def hand_over(out_in, grad_in, weight_in, output, grad_features, grad_weight):
    output[...] = out_in[...]
    grad_features[...] = grad_in[...]
    grad_weight[...] = weight_in[...]


VM = pl.BlockSpec(memory_space=pltpu.VMEM)
SM = pl.BlockSpec(memory_space=pltpu.SMEM)
HBM = pl.BlockSpec(memory_space=pltpu.HBM)
LINKS = 160


def shape(*dims, dtype=BF16):
    return jax.ShapeDtypeStruct(dims, dtype)


def buf(*dims, dtype=BF16):
    return pltpu.VMEM(dims, dtype)


def body(features, weight, tiles, coords, counts, cotangent):
    shapes = (shape(TILE, HID), shape(TILE, HID), shape(HID, HID, dtype=F32))
    results = pl.pallas_call(
        kernel,
        out_shape=shapes,
        in_specs=[VM, SM, HBM, HBM, HBM, HBM],
        out_specs=(VM, VM, VM),
        scratch_shapes=[
            buf(SLOTS + 1, TILE, TILE),
            buf(4, 4, TILE, HID),
            buf(HID, HID),
            buf(TROWS, TILE, HID, dtype=F32),
            buf(4, 4, 2, TILE, HID),
            buf(4, 4, TILE, HID),
            buf(4, 3, TILE, HID),
            buf(4, TILE, HID),
            buf(4, TILE, HID),
            buf(4, 4, 2, HID, TILE),
            buf(TCOLS // 2, HID, HID, dtype=F32),
            buf(4, 4, HID, TILE),
            buf(4, 3, HID, TILE),
            buf(3, HID, TILE),
            buf(4, HID, TILE),
            buf(3, HID, TILE),
            buf(TILE, HID),
            buf(8, 4, 16, 128),
            buf(7, 4, 16, 128),
            buf(4, 16, 128),
            buf(3, 16, 128),
            buf(16, 16, 128),
            buf(4, 16, 128),
            buf(8, 4, 16, 128),
            buf(8, 128, dtype=jnp.int32),
            buf(TROWS, 128, dtype=jnp.int32),
            pltpu.SMEM((TROWS, 128), jnp.int32),
            pltpu.SemaphoreType.DMA((5,)),
            pltpu.SemaphoreType.DMA((LINKS,)),
            pltpu.SemaphoreType.DMA((LINKS,)),
        ],
        compiler_params=pltpu.CompilerParams(
            collective_id=1, has_side_effects=True, vmem_limit_bytes=VMEM_LIMIT
        ),
        name="layer",
    )(coords[0, 0].T, counts, features, weight, tiles[0, 0], cotangent)
    return pl.pallas_call(
        hand_over,
        out_shape=shapes,
        in_specs=[VM] * 3,
        out_specs=(VM,) * 3,
        name="hand_over",
    )(*results)


def solution(mesh):
    placed = (
        P(("col", "row"), None),
        P(),
        P("row", "col", None, None, None),
        P("row", "col", None, None),
        P("row", "col"),
        P(("row", "col"), None),
    )
    return jax.shard_map(
        body,
        mesh=mesh,
        in_specs=placed,
        out_specs=(P(("row", "col"), None), P(("col", "row"), None), P()),
        check_vma=False,
    )
```

```python
import jax
import jax.numpy as jnp
from jax import lax
from jax.experimental import pallas as pl
from jax.experimental.pallas import tpu as pltpu
from jax.sharding import PartitionSpec as P

F32 = jnp.float32
BF16 = jnp.bfloat16
MESH = pl.DeviceIdType.MESH
TILE = 128
HID = 256
TROWS = 32
TCOLS = 16
SLOTS = 96
VMEM_LIMIT = 58 * 2**20


def flip1(v):
    return v + 1 - 2 * lax.rem(v, 2)


def flip2(v):
    return lax.rem(v + 2, 4)


def flip3(v):
    return 3 - v


FLIPS = {0: lambda v: v, 1: flip1, 2: flip2, 3: flip3}


class Place:
    def __init__(self):
        row = lax.axis_index("row")
        col = lax.axis_index("col")
        self.y = lax.div(row, 4)
        self.zh = lax.rem(row, 4)
        self.zl = lax.div(col, 8)
        self.x = lax.rem(lax.div(col, 2), 4)
        self.core = lax.rem(col, 2)

    def peer(self, y=0, zh=0, zl=0, x=0, core=0):
        row = FLIPS[y](self.y) * 4 + FLIPS[zh](self.zh)
        col = FLIPS[zl](self.zl) * 8 + FLIPS[x](self.x) * 2 + FLIPS[core](self.core)
        return (row, col)


class Net:
    def __init__(self, send_sems, recv_sems):
        self.send_sems = send_sems
        self.recv_sems = recv_sems
        self.started = []
        self.finished = 0

    def send(self, src, dst, device):
        i = len(self.started)
        copy = pltpu.make_async_remote_copy(
            src_ref=src,
            dst_ref=dst,
            send_sem=self.send_sems.at[i],
            recv_sem=self.recv_sems.at[i],
            device_id=device,
            device_id_type=MESH,
        )
        copy.start()
        self.started.append(copy)
        return copy

    def finish(self):
        for copy in self.started[self.finished:]:
            copy.wait_send()
        self.finished = len(self.started)


def greet(peers):
    barrier = pltpu.get_barrier_semaphore()
    for peer in peers:
        pl.semaphore_signal(barrier, inc=1, device_id=peer, device_id_type=MESH)
    return lambda: pl.semaphore_wait(barrier, len(peers))


def add(*values):
    total = values[0].astype(F32)
    for value in values[1:]:
        total = total + value.astype(F32)
    return total.astype(BF16)


def ring_gather(net, at, near, far, late=False):
    copies = {}

    def first():
        copies["n0"] = net.send(at(0, 0), at(1, 0), near)
        copies["f1"] = net.send(at(0, 1), at(3, 1), far)
        if not late:
            rest()

    def rest():
        copies["n1"] = net.send(at(0, 1), at(1, 1), near)
        copies["f0"] = net.send(at(0, 0), at(3, 0), far)

    def second():
        copies["n0"].wait_recv()
        copies["nf"] = net.send(at(1, 0), at(2, 0), far)
        copies["f1"].wait_recv()
        copies["fn"] = net.send(at(3, 1), at(2, 1), near)
        copies["n1"].wait_recv()
        copies["f0"].wait_recv()

    def third():
        copies["nf"].wait_recv()
        copies["fn"].wait_recv()

    first.rest = rest
    third.halves = (lambda: copies["nf"].wait_recv(), lambda: copies["fn"].wait_recv())
    return first, second, third


def ring_scatter(net, at, landing, near, far):
    copies = {}

    def first():
        copies["t1"] = net.send(at(2, 0), landing(2, 0), near)
        copies["t3"] = net.send(at(2, 1), landing(2, 1), far)
        copies["n0"] = net.send(at(1, 0), landing(0, 0), near)
        copies["f1"] = net.send(at(3, 1), landing(1, 1), far)

    def second():
        copies["t1"].wait_recv()
        share = at(3, 0)
        share[...] = add(share[...], landing(2, 0)[...])
        copies["f0"] = net.send(share, landing(1, 0), far)
        copies["t3"].wait_recv()
        share = at(1, 1)
        share[...] = add(share[...], landing(2, 1)[...])
        copies["n1"] = net.send(share, landing(0, 1), near)

    def third():
        for name in ("n0", "f1", "f0", "n1"):
            copies[name].wait_recv()

    return first, second, third


def halves(size):
    half = size // 2
    return {0: slice(0, half), 1: slice(half, size), None: slice(None)}


def kernel(
    coords, count, features, weight, tiles, cotangent,
    output, grad_features, grad_weight,
    held, feats, mat, acc, partial, from_core, from_x, total_x, from_z,
    grads, back_acc, back, from_y, direct_y, total_y, from_zh,
    cot, shares, got8, sum8, got16, pair, all4, all8, activated, summed_weight, spots, places, slots,
    local_sems, send_sems, recv_sems,
):
    place = Place()
    net = Net(send_sems, recv_sems)
    node = halves(TILE)
    wide = halves(HID)

    y_peers = {i: place.peer(y=i) for i in (1, 2, 3)}
    z_peers = {i: place.peer(zh=i) for i in (1, 3)}
    along = {i: place.peer(zl=i) for i in (1, 2, 3)}
    yz_pairs = [(i, j) for i in range(4) for j in range(4) if i or j]
    yz_peers = {pair: place.peer(y=pair[0], zl=pair[1]) for pair in yz_pairs}
    x_pairs = [(i, j) for i in range(4) for j in range(2) if i or j]
    x_peers = {pair: place.peer(x=pair[0], core=pair[1]) for pair in x_pairs}
    load_feats = pltpu.make_async_copy(features, feats.at[0, 0], local_sems.at[0])
    load_feats.start()
    partners = [*z_peers.values(), *yz_peers.values(), *x_peers.values()]
    arrived = greet(partners)
    load_weight = pltpu.make_async_copy(weight, mat, local_sems.at[1])
    load_tiles = pltpu.make_async_copy(tiles, held.at[pl.ds(0, SLOTS)], local_sems.at[2])
    load_cot = pltpu.make_async_copy(cotangent, cot, local_sems.at[3])
    for copy in (load_tiles, load_weight, load_cot):
        copy.start()

    zh_near, zh_far = z_peers[1], z_peers[3]
    y_near, y_far = y_peers[1], y_peers[3]
    x_near, x_far = x_peers[(1, 0)], x_peers[(3, 0)]
    other = x_peers[(0, 1)]

    def at_zh(i, half):
        return feats.at[0, i, node[half]]

    def at_y(k):
        return lambda i, half: feats.at[i, k, node[half]]

    load_feats.wait()
    arrived()
    z_ring = ring_gather(net, at_zh, zh_near, zh_far, late=True)
    rings = {k: ring_gather(net, at_y(k), y_near, y_far) for k in (0, 1, 3)}
    z_ring[0]()
    rings[0][0]()

    spots[...] = jnp.zeros((8, 128), jnp.int32)
    spots[0:2, 0:SLOTS] = coords[...]
    far_row = jnp.broadcast_to(spots[0:1, :], (128, 128)).T[:SLOTS] ^ lax.axis_index("col")
    far_col = jnp.broadcast_to(spots[1:2, :], (128, 128)).T[:SLOTS] ^ lax.axis_index("row")
    slot = lax.broadcasted_iota(jnp.int32, (SLOTS, 128), 0)
    lane = lax.broadcasted_iota(jnp.int32, (SLOTS, 128), 1)
    value = jnp.where((far_col == lane) & (slot < count[0, 0]), slot - SLOTS, 0)
    for t in range(TROWS):
        found = jnp.where(far_row == t, value, 0)
        places[t:t + 1] = SLOTS + jnp.sum(found, axis=0, keepdims=True)
    load_slots = pltpu.make_async_copy(places, slots, local_sems.at[4])
    load_slots.start()
    z_ring[0].rest()
    held[SLOTS] = jnp.zeros((TILE, TILE), BF16)

    def forward(targets, ks):
        places = [(i, k) for k in ks for i in range(4)]
        left = jnp.concatenate(
            [
                jnp.concatenate([held[slots[t, i * 4 + k]] for i, k in places], axis=1)
                for t in targets
            ],
            axis=0,
        )
        right = jnp.concatenate([feats[i, k] for i, k in places], axis=0)
        return jnp.dot(left, right, preferred_element_type=F32)

    def sweep(ks, first):
        def block(b, carry):
            targets = [b * 4 + i for i in range(4)]
            value = forward(targets, ks).reshape(4, TILE, HID)
            rows = pl.ds(b * 4, 4)
            acc[rows] = value if first else acc[rows] + value
            return carry

        lax.fori_loop(0, TROWS // 4, block, 0)

    z_ring[1]()
    rings[1][0]()
    rings[3][0]()
    rings[0][1]()
    rings[0][2]()
    load_tiles.wait()
    load_slots.wait()
    sweep((0,), True)
    rings[1][1]()
    rings[3][1]()
    direct = []
    for wait, half in zip(z_ring[2].halves, (0, 1)):
        wait()
        for i in (2, 1, 3):
            direct.append(net.send(at_zh(2, half), at_y(2)(i, half), y_peers[i]))
    rings[1][2]()
    rings[3][2]()
    sweep((1, 3), False)
    for copy in direct:
        copy.wait_recv()

    order = (3, 2, 1, 0)

    def finish_block(k, core):
        targets = [k * 8 + x * 2 + core for x in range(4)]
        value = forward(targets, (2,))
        for x, t in enumerate(targets):
            rows = slice(x * TILE, (x + 1) * TILE)
            partial[k, x, core] = (acc[t] + value[rows]).astype(BF16)

    core_copies = {}

    def give_core(k):
        finish_block(k, 1)
        core_copies[k] = net.send(partial.at[k, :, 1], from_core.at[k], other)

    def at_x(k):
        return lambda i, half: from_core.at[k, i, node[half]]

    def land_x(k):
        return lambda i, half: from_x.at[k, i, node[half]]

    rings = {k: ring_scatter(net, at_x(k), land_x(k), x_near, x_far) for k in order}
    z_copies = {}

    def start(k):
        core_copies[k].wait_recv()
        for i in (2, 1, 3):
            from_core[k, i] = add(from_core[k, i], partial[k, i, 0])
        rings[k][0]()

    def close(k):
        rings[k][2]()
        parts = (partial[k, 0, 0], from_core[k, 0], from_x[k, 0], from_x[k, 1])
        if k:
            total_x[k] = add(*parts)
            z_copies[k] = net.send(total_x.at[k], from_z.at[k], along[k])
            return None
        return sum(part.astype(F32) for part in parts)

    give_core(3)
    finish_block(3, 0)
    give_core(2)
    start(3)
    finish_block(2, 0)
    give_core(1)
    start(2)
    finish_block(1, 0)
    rings[3][1]()
    give_core(0)
    start(1)
    finish_block(0, 0)
    rings[2][1]()
    start(0)
    close(3)
    rings[1][1]()
    close(2)
    rings[0][1]()
    close(1)
    own = close(0)
    load_cot.wait()
    load_weight.wait()
    for k in (3, 2, 1):
        z_copies[k].wait_recv()
        own = own + from_z[k].astype(F32)
    summed = own.astype(BF16)
    hidden = jnp.dot(summed, mat[...], preferred_element_type=F32)
    sig = jax.nn.sigmoid(hidden)
    slope = sig * (1.0 + hidden * (1.0 - sig))
    grads[0, 0, 0] = (cot[...].astype(F32) * slope).T.astype(BF16)

    out_copies = {k: net.send(grads.at[0, 0, 0], grads.at[k, 0, 0], along[k]) for k in (1, 2, 3)}

    def at_g(k):
        return lambda i, half: grads.at[k, i, 0, wide[half]]

    rounds = {k: ring_gather(net, at_g(k), x_near, x_far) for k in range(4)}
    rounds[0][0]()
    last = {}

    def unpacked(p, q):
        rows = p * 32 + (q // 2) * 16
        lanes = (q % 2) * 128
        return slice(rows, rows + 16), slice(lanes, lanes + 128)

    me8 = place.x * 2 + place.core
    sums = {}
    save_weight = pltpu.make_async_copy(summed_weight, grad_weight, local_sems.at[6])

    def sum_start():
        term = jnp.dot(grads[0, 0, 0], summed, preferred_element_type=F32).astype(BF16)
        for p in range(8):
            for q in range(4):
                rows, lanes = unpacked(p, q)
                shares[p, q] = term[rows, lanes]
        sums[0] = [
            net.send(
                shares.at[FLIPS[i](place.x) * 2 + FLIPS[j](place.core)],
                got8.at[n], x_peers[(i, j)],
            )
            for n, (i, j) in enumerate(x_pairs)
        ]

    def sum_8():
        total = shares[me8].astype(F32)
        for n, copy in enumerate(sums[0]):
            copy.wait_recv()
            total = total + got8[n].astype(F32)
        sum8[...] = total.astype(BF16)
        got16[place.y, place.zl] = sum8[place.y]
        sums[1] = [
            net.send(
                sum8.at[FLIPS[i](place.y)], got16.at[place.y, place.zl], yz_peers[(i, j)]
            )
            for i, j in yz_pairs
        ]

    def sum_16():
        for copy in sums[1]:
            copy.wait_recv()
        pair[0] = add(*(got16[i, j] for i in range(4) for j in range(4)))
        sums[3] = net.send(pair.at[0], pair.at[1], zh_near)

    def sum_near():
        sums[3].wait_recv()
        pair[2] = add(pair[0], pair[1])
        sums[4] = net.send(pair.at[2], pair.at[3], zh_far)

    def sum_far():
        sums[4].wait_recv()
        all4[place.y] = add(pair[2], pair[3])
        sums[5] = [net.send(all4.at[place.y], all4.at[place.y], y_peers[i]) for i in (1, 2, 3)]

    def spread_4():
        for copy in sums[5]:
            copy.wait_recv()
        sums[6] = [net.send(all4, all8.at[me8], x_peers[pair]) for pair in x_pairs]
        all8[me8] = all4[...]

    def sum_end():
        for copy in sums[6]:
            copy.wait_recv()
        rows = [
            jnp.concatenate([all8[p, q].astype(F32), all8[p, q + 1].astype(F32)], axis=1)
            for p in range(8) for q in (0, 2)
        ]
        summed_weight[...] = jnp.concatenate(rows, axis=0).T
        save_weight.start()

    def swap(k):
        rounds[k][2]()
        last[k] = net.send(grads.at[k, :, 0], grads.at[k, :, 1], other)

    def backward(k, p):
        left = jnp.concatenate([grads[k, x, c] for x in range(4) for c in range(2)], axis=1)
        right = jnp.concatenate(
            [
                jnp.concatenate(
                    [held[slots[k * 8 + j, 2 * p + i]] for i in range(2)], axis=1
                )
                for j in range(8)
            ],
            axis=0,
        )
        return jnp.dot(left, right, preferred_element_type=F32)

    def back_sweep(k, first):
        last[k].wait_recv()

        def block(p, carry):
            value = backward(k, p)
            back_acc[p] = value if first else back_acc[p] + value
            return carry

        lax.fori_loop(0, TCOLS // 2, block, 0)

    sum_start()
    out_copies[1].wait_recv()
    rounds[1][0]()
    rounds[0][1]()
    activated[...] = (hidden * sig).astype(BF16)
    save_output = pltpu.make_async_copy(activated, output, local_sems.at[5])
    save_output.start()
    out_copies[2].wait_recv()
    rounds[2][0]()
    sum_8()
    rounds[1][1]()
    swap(0)
    out_copies[3].wait_recv()
    rounds[3][0]()
    rounds[2][1]()
    swap(1)
    back_sweep(0, True)
    rounds[3][1]()
    sum_16()
    swap(2)
    back_sweep(1, False)
    swap(3)
    back_sweep(2, False)
    sum_near()
    last[3].wait_recv()

    def at_b(k):
        return lambda i, half: back.at[i, k, wide[half]]

    def land_y(k):
        return lambda i, half: from_y.at[k, i, wide[half]]

    rings = {k: ring_scatter(net, at_b(k), land_y(k), y_near, y_far) for k in (0, 1, 3)}

    def back_pairs(pair):
        def block(i, carry):
            p = i * 2 + pair
            value = (back_acc[p] + backward(3, p)).astype(BF16)
            back[i, 2 * pair] = value[:, :TILE]
            back[i, 2 * pair + 1] = value[:, TILE:]
            return carry

        lax.fori_loop(0, 4, block, 0)

    def zh_send(k, slot, half, peer):
        return net.send(total_y.at[k, wide[half]], from_zh.at[slot, wide[half]], peer)

    def close_y(k):
        rings[k][2]()
        total_y[k] = add(back[0, k], from_y[k, 0], from_y[k, 1])

    back_pairs(1)
    direct = {
        half: [net.send(at_b(2)(i, half), direct_y.at[i - 1, wide[half]], y_peers[i]) for i in (2, 1, 3)]
        for half in (0, 1)
    }
    rings[3][0]()
    back_pairs(0)
    rings[1][0]()
    rings[0][0]()
    transit = {}
    for half, peer in ((0, zh_near), (1, zh_far)):
        for copy in direct[half]:
            copy.wait_recv()
        rows = wide[half]
        total_y[2, rows] = add(
            back[0, 2, rows], direct_y[0, rows], direct_y[1, rows], direct_y[2, rows]
        )
        transit[half] = zh_send(2, 2, half, peer)
    rings[3][1]()
    rings[1][1]()
    rings[0][1]()
    sum_far()
    close_y(3)
    far1 = zh_send(3, 1, 1, zh_far)
    close_y(1)
    near0 = zh_send(1, 0, 0, zh_near)
    transit[0].wait_recv()
    total_y[3, wide[0]] = add(total_y[3, wide[0]], from_zh[2, wide[0]])
    far0 = zh_send(3, 1, 0, zh_far)
    spread_4()
    transit[1].wait_recv()
    total_y[1, wide[1]] = add(total_y[1, wide[1]], from_zh[2, wide[1]])
    near1 = zh_send(1, 0, 1, zh_near)
    rings[0][2]()
    own = back[0, 0].astype(F32) + from_y[0, 0].astype(F32) + from_y[0, 1].astype(F32)
    sum_end()
    net.finish()
    for copy in (near0, far1, far0, near1):
        copy.wait_recv()
    own = own + from_zh[0].astype(F32) + from_zh[1].astype(F32)
    grad_features[...] = lax.dot_general(
        own.T.astype(BF16), mat[...], (((1,), (1,)), ((), ())), preferred_element_type=F32
    ).astype(BF16)
    net.finish()
    save_output.wait()
    save_weight.wait()


def hand_over(out_in, grad_in, weight_in, output, grad_features, grad_weight):
    output[...] = out_in[...]
    grad_features[...] = grad_in[...]
    grad_weight[...] = weight_in[...]


VM = pl.BlockSpec(memory_space=pltpu.VMEM)
SM = pl.BlockSpec(memory_space=pltpu.SMEM)
HBM = pl.BlockSpec(memory_space=pltpu.HBM)
LINKS = 160


def shape(*dims, dtype=BF16):
    return jax.ShapeDtypeStruct(dims, dtype)


def buf(*dims, dtype=BF16):
    return pltpu.VMEM(dims, dtype)


def body(features, weight, tiles, coords, counts, cotangent):
    shapes = (shape(TILE, HID), shape(TILE, HID), shape(HID, HID, dtype=F32))
    results = pl.pallas_call(
        kernel,
        out_shape=shapes,
        in_specs=[VM, SM, HBM, HBM, HBM, HBM],
        out_specs=(HBM, VM, HBM),
        scratch_shapes=[
            buf(SLOTS + 1, TILE, TILE),
            buf(4, 4, TILE, HID),
            buf(HID, HID),
            buf(TROWS, TILE, HID, dtype=F32),
            buf(4, 4, 2, TILE, HID),
            buf(4, 4, TILE, HID),
            buf(4, 3, TILE, HID),
            buf(4, TILE, HID),
            buf(4, TILE, HID),
            buf(4, 4, 2, HID, TILE),
            buf(TCOLS // 2, HID, HID, dtype=F32),
            buf(4, 4, HID, TILE),
            buf(4, 3, HID, TILE),
            buf(3, HID, TILE),
            buf(4, HID, TILE),
            buf(3, HID, TILE),
            buf(TILE, HID),
            buf(8, 4, 16, 128),
            buf(7, 4, 16, 128),
            buf(4, 16, 128),
            buf(4, 4, 16, 128),
            buf(4, 16, 128),
            buf(4, 16, 128),
            buf(8, 4, 16, 128),
            buf(TILE, HID),
            buf(HID, HID, dtype=F32),
            buf(8, 128, dtype=jnp.int32),
            buf(TROWS, 128, dtype=jnp.int32),
            pltpu.SMEM((TROWS, 128), jnp.int32),
            pltpu.SemaphoreType.DMA((7,)),
            pltpu.SemaphoreType.DMA((LINKS,)),
            pltpu.SemaphoreType.DMA((LINKS,)),
        ],
        compiler_params=pltpu.CompilerParams(
            collective_id=1, has_side_effects=True, vmem_limit_bytes=VMEM_LIMIT
        ),
        name="layer",
    )(coords[0, 0].T, counts, features, weight, tiles[0, 0], cotangent)
    return pl.pallas_call(
        hand_over,
        out_shape=shapes,
        in_specs=[VM] * 3,
        out_specs=(VM,) * 3,
        name="hand_over",
    )(*results)


def solution(mesh):
    placed = (
        P(("col", "row"), None),
        P(),
        P("row", "col", None, None, None),
        P("row", "col", None, None),
        P("row", "col"),
        P(("row", "col"), None),
    )
    return jax.shard_map(
        body,
        mesh=mesh,
        in_specs=placed,
        out_specs=(P(("row", "col"), None), P(("col", "row"), None), P()),
        check_vma=False,
    )
```

```python
import jax
import jax.numpy as jnp
from jax import lax
from jax.experimental import pallas as pl
from jax.experimental.pallas import tpu as pltpu
from jax.sharding import PartitionSpec as P

F32 = jnp.float32
BF16 = jnp.bfloat16
MESH = pl.DeviceIdType.MESH
TILE = 128
HID = 256
TROWS = 32
TCOLS = 16
SLOTS = 96
VMEM_LIMIT = 58 * 2**20


def flip1(v):
    return v + 1 - 2 * lax.rem(v, 2)


def flip2(v):
    return lax.rem(v + 2, 4)


def flip3(v):
    return 3 - v


FLIPS = {0: lambda v: v, 1: flip1, 2: flip2, 3: flip3}


class Place:
    def __init__(self):
        row = lax.axis_index("row")
        col = lax.axis_index("col")
        self.y = lax.div(row, 4)
        self.zh = lax.rem(row, 4)
        self.zl = lax.div(col, 8)
        self.x = lax.rem(lax.div(col, 2), 4)
        self.core = lax.rem(col, 2)

    def peer(self, y=0, zh=0, zl=0, x=0, core=0):
        row = FLIPS[y](self.y) * 4 + FLIPS[zh](self.zh)
        col = FLIPS[zl](self.zl) * 8 + FLIPS[x](self.x) * 2 + FLIPS[core](self.core)
        return (row, col)


class Net:
    def __init__(self, send_sems, recv_sems):
        self.send_sems = send_sems
        self.recv_sems = recv_sems
        self.started = []
        self.finished = 0

    def send(self, src, dst, device):
        i = len(self.started)
        copy = pltpu.make_async_remote_copy(
            src_ref=src,
            dst_ref=dst,
            send_sem=self.send_sems.at[i],
            recv_sem=self.recv_sems.at[i],
            device_id=device,
            device_id_type=MESH,
        )
        copy.start()
        self.started.append(copy)
        return copy

    def finish(self):
        for copy in self.started[self.finished:]:
            copy.wait_send()
        self.finished = len(self.started)


def greet(peers):
    barrier = pltpu.get_barrier_semaphore()
    for peer in peers:
        pl.semaphore_signal(barrier, inc=1, device_id=peer, device_id_type=MESH)
    return lambda: pl.semaphore_wait(barrier, len(peers))


def add(*values):
    total = values[0].astype(F32)
    for value in values[1:]:
        total = total + value.astype(F32)
    return total.astype(BF16)


def ring_gather(net, at, near, far, late=False):
    copies = {}

    def first():
        copies["n0"] = net.send(at(0, 0), at(1, 0), near)
        copies["f1"] = net.send(at(0, 1), at(3, 1), far)
        if not late:
            rest()

    def rest():
        copies["n1"] = net.send(at(0, 1), at(1, 1), near)
        copies["f0"] = net.send(at(0, 0), at(3, 0), far)

    def second():
        copies["n0"].wait_recv()
        copies["nf"] = net.send(at(1, 0), at(2, 0), far)
        copies["f1"].wait_recv()
        copies["fn"] = net.send(at(3, 1), at(2, 1), near)
        copies["n1"].wait_recv()
        copies["f0"].wait_recv()

    def third():
        copies["nf"].wait_recv()
        copies["fn"].wait_recv()

    first.rest = rest
    third.halves = (lambda: copies["nf"].wait_recv(), lambda: copies["fn"].wait_recv())
    return first, second, third


def ring_scatter(net, at, landing, near, far):
    copies = {}

    def first():
        copies["t1"] = net.send(at(2, 0), landing(2, 0), near)
        copies["t3"] = net.send(at(2, 1), landing(2, 1), far)
        copies["n0"] = net.send(at(1, 0), landing(0, 0), near)
        copies["f1"] = net.send(at(3, 1), landing(1, 1), far)

    def second():
        copies["t1"].wait_recv()
        share = at(3, 0)
        share[...] = add(share[...], landing(2, 0)[...])
        copies["f0"] = net.send(share, landing(1, 0), far)
        copies["t3"].wait_recv()
        share = at(1, 1)
        share[...] = add(share[...], landing(2, 1)[...])
        copies["n1"] = net.send(share, landing(0, 1), near)

    def third():
        for name in ("n0", "f1", "f0", "n1"):
            copies[name].wait_recv()

    return first, second, third


def halves(size):
    half = size // 2
    return {0: slice(0, half), 1: slice(half, size), None: slice(None)}


def kernel(
    coords, count, features, weight, tiles, cotangent,
    output, grad_features, grad_weight,
    held, feats, mat, acc, partial, from_core, from_x, total_x, from_z,
    grads, back_acc, back, from_y, direct_y, total_y, from_zh,
    cot, shares, got8, sum8, got16, pair, all4, all8, activated, summed_weight, spots, places, slots,
    local_sems, send_sems, recv_sems,
):
    place = Place()
    net = Net(send_sems, recv_sems)
    node = halves(TILE)
    wide = halves(HID)

    y_peers = {i: place.peer(y=i) for i in (1, 2, 3)}
    z_peers = {i: place.peer(zh=i) for i in (1, 3)}
    along = {i: place.peer(zl=i) for i in (1, 2, 3)}
    yz_pairs = [(i, j) for i in range(4) for j in range(4) if i or j]
    yz_peers = {pair: place.peer(y=pair[0], zl=pair[1]) for pair in yz_pairs}
    x_pairs = [(i, j) for i in range(4) for j in range(2) if i or j]
    x_peers = {pair: place.peer(x=pair[0], core=pair[1]) for pair in x_pairs}
    load_feats = pltpu.make_async_copy(features, feats.at[0, 0], local_sems.at[0])
    load_feats.start()
    partners = [*z_peers.values(), *yz_peers.values(), *x_peers.values()]
    arrived = greet(partners)
    load_weight = pltpu.make_async_copy(weight, mat, local_sems.at[1])
    load_tiles = pltpu.make_async_copy(tiles, held.at[pl.ds(0, SLOTS)], local_sems.at[2])
    load_cot = pltpu.make_async_copy(cotangent, cot, local_sems.at[3])
    for copy in (load_tiles, load_weight, load_cot):
        copy.start()

    zh_near, zh_far = z_peers[1], z_peers[3]
    y_near, y_far = y_peers[1], y_peers[3]
    x_near, x_far = x_peers[(1, 0)], x_peers[(3, 0)]
    other = x_peers[(0, 1)]

    def at_zh(i, half):
        return feats.at[0, i, node[half]]

    def at_y(k):
        return lambda i, half: feats.at[i, k, node[half]]

    load_feats.wait()
    arrived()
    z_ring = ring_gather(net, at_zh, zh_near, zh_far, late=True)
    rings = {k: ring_gather(net, at_y(k), y_near, y_far) for k in (0, 1, 3)}
    z_ring[0]()
    rings[0][0]()

    spots[...] = jnp.zeros((8, 128), jnp.int32)
    spots[0:2, 0:SLOTS] = coords[...]
    far_row = jnp.broadcast_to(spots[0:1, :], (128, 128)).T[:SLOTS] ^ lax.axis_index("col")
    far_col = jnp.broadcast_to(spots[1:2, :], (128, 128)).T[:SLOTS] ^ lax.axis_index("row")
    slot = lax.broadcasted_iota(jnp.int32, (SLOTS, 128), 0)
    lane = lax.broadcasted_iota(jnp.int32, (SLOTS, 128), 1)
    value = jnp.where((far_col == lane) & (slot < count[0, 0]), slot - SLOTS, 0)
    for t in range(TROWS):
        found = jnp.where(far_row == t, value, 0)
        places[t:t + 1] = SLOTS + jnp.sum(found, axis=0, keepdims=True)
    load_slots = pltpu.make_async_copy(places, slots, local_sems.at[4])
    load_slots.start()
    z_ring[0].rest()
    held[SLOTS] = jnp.zeros((TILE, TILE), BF16)

    def forward(targets, ks):
        places = [(i, k) for k in ks for i in range(4)]
        left = jnp.concatenate(
            [
                jnp.concatenate([held[slots[t, i * 4 + k]] for i, k in places], axis=1)
                for t in targets
            ],
            axis=0,
        )
        right = jnp.concatenate([feats[i, k] for i, k in places], axis=0)
        return jnp.dot(left, right, preferred_element_type=F32)

    def sweep(ks, first):
        def block(b, carry):
            targets = [b * 4 + i for i in range(4)]
            value = forward(targets, ks).reshape(4, TILE, HID)
            rows = pl.ds(b * 4, 4)
            acc[rows] = value if first else acc[rows] + value
            return carry

        lax.fori_loop(0, TROWS // 4, block, 0)

    z_ring[1]()
    rings[1][0]()
    rings[3][0]()
    rings[0][1]()
    rings[0][2]()
    load_tiles.wait()
    load_slots.wait()
    sweep((0,), True)
    rings[1][1]()
    rings[3][1]()
    direct = []
    for wait, half in zip(z_ring[2].halves, (0, 1)):
        wait()
        for i in (2, 1, 3):
            direct.append(net.send(at_zh(2, half), at_y(2)(i, half), y_peers[i]))
    rings[1][2]()
    rings[3][2]()
    sweep((1, 3), False)
    for copy in direct:
        copy.wait_recv()

    order = (3, 2, 1, 0)

    def finish_block(k, core):
        targets = [k * 8 + x * 2 + core for x in range(4)]
        value = forward(targets, (2,))
        for x, t in enumerate(targets):
            rows = slice(x * TILE, (x + 1) * TILE)
            partial[k, x, core] = (acc[t] + value[rows]).astype(BF16)

    core_copies = {}

    def give_core(k):
        finish_block(k, 1)
        core_copies[k] = net.send(partial.at[k, :, 1], from_core.at[k], other)

    def at_x(k):
        return lambda i, half: from_core.at[k, i, node[half]]

    def land_x(k):
        return lambda i, half: from_x.at[k, i, node[half]]

    rings = {k: ring_scatter(net, at_x(k), land_x(k), x_near, x_far) for k in order}
    z_copies = {}

    def start(k):
        core_copies[k].wait_recv()
        for i in (2, 1, 3):
            from_core[k, i] = add(from_core[k, i], partial[k, i, 0])
        rings[k][0]()

    def close(k):
        rings[k][2]()
        parts = (partial[k, 0, 0], from_core[k, 0], from_x[k, 0], from_x[k, 1])
        if k:
            total_x[k] = add(*parts)
            z_copies[k] = net.send(total_x.at[k], from_z.at[k], along[k])
            return None
        return sum(part.astype(F32) for part in parts)

    give_core(3)
    finish_block(3, 0)
    give_core(2)
    start(3)
    finish_block(2, 0)
    give_core(1)
    start(2)
    finish_block(1, 0)
    rings[3][1]()
    give_core(0)
    start(1)
    finish_block(0, 0)
    rings[2][1]()
    start(0)
    close(3)
    rings[1][1]()
    close(2)
    rings[0][1]()
    close(1)
    own = close(0)
    load_cot.wait()
    load_weight.wait()
    for k in (3, 2, 1):
        z_copies[k].wait_recv()
        own = own + from_z[k].astype(F32)
    summed = own.astype(BF16)
    hidden = jnp.dot(summed, mat[...], preferred_element_type=F32)
    sig = jax.nn.sigmoid(hidden)
    slope = sig * (1.0 + hidden * (1.0 - sig))
    grads[0, 0, 0] = (cot[...].astype(F32) * slope).T.astype(BF16)

    out_copies = {k: net.send(grads.at[0, 0, 0], grads.at[k, 0, 0], along[k]) for k in (1, 2, 3)}

    def at_g(k):
        return lambda i, half: grads.at[k, i, 0, wide[half]]

    rounds = {k: ring_gather(net, at_g(k), x_near, x_far) for k in range(4)}
    rounds[0][0]()
    last = {}

    def unpacked(p, q):
        rows = p * 32 + (q // 2) * 16
        lanes = (q % 2) * 128
        return slice(rows, rows + 16), slice(lanes, lanes + 128)

    me8 = place.x * 2 + place.core
    sums = {}
    save_weight = pltpu.make_async_copy(summed_weight, grad_weight, local_sems.at[6])

    def sum_start():
        term = jnp.dot(grads[0, 0, 0], summed, preferred_element_type=F32).astype(BF16)
        for p in range(8):
            for q in range(4):
                rows, lanes = unpacked(p, q)
                shares[p, q] = term[rows, lanes]
        sums[0] = [
            net.send(
                shares.at[FLIPS[i](place.x) * 2 + FLIPS[j](place.core)],
                got8.at[n], x_peers[(i, j)],
            )
            for n, (i, j) in enumerate(x_pairs)
        ]

    def sum_8():
        total = shares[me8].astype(F32)
        for n, copy in enumerate(sums[0]):
            copy.wait_recv()
            total = total + got8[n].astype(F32)
        sum8[...] = total.astype(BF16)
        got16[place.y, place.zl] = sum8[place.y]
        sums[1] = [
            net.send(
                sum8.at[FLIPS[i](place.y)], got16.at[place.y, place.zl], yz_peers[(i, j)]
            )
            for i, j in yz_pairs
        ]

    def sum_16():
        for copy in sums[1]:
            copy.wait_recv()
        pair[0] = add(*(got16[i, j] for i in range(4) for j in range(4)))
        sums[3] = net.send(pair.at[0], pair.at[1], zh_near)

    def sum_near():
        sums[3].wait_recv()
        pair[2] = add(pair[0], pair[1])
        sums[4] = net.send(pair.at[2], pair.at[3], zh_far)

    def sum_far():
        sums[4].wait_recv()
        all4[place.y] = add(pair[2], pair[3])
        sums[5] = [net.send(all4.at[place.y], all4.at[place.y], y_peers[i]) for i in (1, 2, 3)]

    def spread_4():
        for copy in sums[5]:
            copy.wait_recv()
        sums[6] = [net.send(all4, all8.at[me8], x_peers[pair]) for pair in x_pairs]
        all8[me8] = all4[...]

    def sum_end():
        for copy in sums[6]:
            copy.wait_recv()
        rows = [
            jnp.concatenate([all8[p, q].astype(F32), all8[p, q + 1].astype(F32)], axis=1)
            for p in range(8) for q in (0, 2)
        ]
        summed_weight[...] = jnp.concatenate(rows, axis=0).T
        save_weight.start()

    def swap(k):
        rounds[k][2]()
        last[k] = net.send(grads.at[k, :, 0], grads.at[k, :, 1], other)

    def backward(k, p):
        left = jnp.concatenate([grads[k, x, c] for x in range(4) for c in range(2)], axis=1)
        right = jnp.concatenate(
            [
                jnp.concatenate(
                    [held[slots[k * 8 + j, 2 * p + i]] for i in range(2)], axis=1
                )
                for j in range(8)
            ],
            axis=0,
        )
        return jnp.dot(left, right, preferred_element_type=F32)

    def back_sweep(k, first):
        last[k].wait_recv()

        def block(p, carry):
            value = backward(k, p)
            back_acc[p] = value if first else back_acc[p] + value
            return carry

        lax.fori_loop(0, TCOLS // 2, block, 0)

    sum_start()
    out_copies[1].wait_recv()
    rounds[1][0]()
    rounds[0][1]()
    activated[...] = (hidden * sig).astype(BF16)
    save_output = pltpu.make_async_copy(activated, output, local_sems.at[5])
    save_output.start()
    out_copies[2].wait_recv()
    rounds[2][0]()
    sum_8()
    rounds[1][1]()
    swap(0)
    out_copies[3].wait_recv()
    rounds[3][0]()
    rounds[2][1]()
    swap(1)
    back_sweep(0, True)
    rounds[3][1]()
    sum_16()
    swap(2)
    back_sweep(1, False)
    swap(3)
    back_sweep(2, False)
    sum_near()
    last[3].wait_recv()

    def at_b(k):
        return lambda i, half: back.at[i, k, wide[half]]

    def land_y(k):
        return lambda i, half: from_y.at[k, i, wide[half]]

    rings = {k: ring_scatter(net, at_b(k), land_y(k), y_near, y_far) for k in (0, 1, 3)}

    def back_pairs(pair):
        def block(i, carry):
            p = i * 2 + pair
            value = (back_acc[p] + backward(3, p)).astype(BF16)
            back[i, 2 * pair] = value[:, :TILE]
            back[i, 2 * pair + 1] = value[:, TILE:]
            return carry

        lax.fori_loop(0, 4, block, 0)

    def zh_send(k, slot, half, peer):
        return net.send(total_y.at[k, wide[half]], from_zh.at[slot, wide[half]], peer)

    def close_y(k):
        rings[k][2]()
        total_y[k] = add(back[0, k], from_y[k, 0], from_y[k, 1])

    def back_pair(i, pair_of):
        p = i * 2 + pair_of
        value = (back_acc[p] + backward(3, p)).astype(BF16)
        back[i, 2 * pair_of] = value[:, :TILE]
        back[i, 2 * pair_of + 1] = value[:, TILE:]

    direct = {0: [], 1: []}
    for i in (2, 1, 3):
        back_pair(i, 1)
        for half in (0, 1):
            direct[half].append(
                net.send(at_b(2)(i, half), direct_y.at[i - 1, wide[half]], y_peers[i])
            )
    rings[3][0]()
    back_pair(0, 1)
    back_pairs(0)
    rings[1][0]()
    rings[0][0]()
    transit = {}
    for half, peer in ((0, zh_near), (1, zh_far)):
        for copy in direct[half]:
            copy.wait_recv()
        rows = wide[half]
        total_y[2, rows] = add(
            back[0, 2, rows], direct_y[0, rows], direct_y[1, rows], direct_y[2, rows]
        )
        transit[half] = zh_send(2, 2, half, peer)
    rings[3][1]()
    rings[1][1]()
    rings[0][1]()
    sum_far()
    close_y(3)
    far1 = zh_send(3, 1, 1, zh_far)
    close_y(1)
    near0 = zh_send(1, 0, 0, zh_near)
    transit[0].wait_recv()
    total_y[3, wide[0]] = add(total_y[3, wide[0]], from_zh[2, wide[0]])
    far0 = zh_send(3, 1, 0, zh_far)
    spread_4()
    transit[1].wait_recv()
    total_y[1, wide[1]] = add(total_y[1, wide[1]], from_zh[2, wide[1]])
    near1 = zh_send(1, 0, 1, zh_near)
    rings[0][2]()
    own = back[0, 0].astype(F32) + from_y[0, 0].astype(F32) + from_y[0, 1].astype(F32)
    sum_end()
    net.finish()
    for copy in (near0, far1, far0, near1):
        copy.wait_recv()
    own = own + from_zh[0].astype(F32) + from_zh[1].astype(F32)
    grad_features[...] = lax.dot_general(
        own.T.astype(BF16), mat[...], (((1,), (1,)), ((), ())), preferred_element_type=F32
    ).astype(BF16)
    net.finish()
    save_output.wait()
    save_weight.wait()


def hand_over(out_in, grad_in, weight_in, output, grad_features, grad_weight):
    output[...] = out_in[...]
    grad_features[...] = grad_in[...]
    grad_weight[...] = weight_in[...]


VM = pl.BlockSpec(memory_space=pltpu.VMEM)
SM = pl.BlockSpec(memory_space=pltpu.SMEM)
HBM = pl.BlockSpec(memory_space=pltpu.HBM)
LINKS = 160


def shape(*dims, dtype=BF16):
    return jax.ShapeDtypeStruct(dims, dtype)


def buf(*dims, dtype=BF16):
    return pltpu.VMEM(dims, dtype)


def body(features, weight, tiles, coords, counts, cotangent):
    shapes = (shape(TILE, HID), shape(TILE, HID), shape(HID, HID, dtype=F32))
    results = pl.pallas_call(
        kernel,
        out_shape=shapes,
        in_specs=[VM, SM, HBM, HBM, HBM, HBM],
        out_specs=(HBM, VM, HBM),
        scratch_shapes=[
            buf(SLOTS + 1, TILE, TILE),
            buf(4, 4, TILE, HID),
            buf(HID, HID),
            buf(TROWS, TILE, HID, dtype=F32),
            buf(4, 4, 2, TILE, HID),
            buf(4, 4, TILE, HID),
            buf(4, 3, TILE, HID),
            buf(4, TILE, HID),
            buf(4, TILE, HID),
            buf(4, 4, 2, HID, TILE),
            buf(TCOLS // 2, HID, HID, dtype=F32),
            buf(4, 4, HID, TILE),
            buf(4, 3, HID, TILE),
            buf(3, HID, TILE),
            buf(4, HID, TILE),
            buf(3, HID, TILE),
            buf(TILE, HID),
            buf(8, 4, 16, 128),
            buf(7, 4, 16, 128),
            buf(4, 16, 128),
            buf(4, 4, 16, 128),
            buf(4, 16, 128),
            buf(4, 16, 128),
            buf(8, 4, 16, 128),
            buf(TILE, HID),
            buf(HID, HID, dtype=F32),
            buf(8, 128, dtype=jnp.int32),
            buf(TROWS, 128, dtype=jnp.int32),
            pltpu.SMEM((TROWS, 128), jnp.int32),
            pltpu.SemaphoreType.DMA((7,)),
            pltpu.SemaphoreType.DMA((LINKS,)),
            pltpu.SemaphoreType.DMA((LINKS,)),
        ],
        compiler_params=pltpu.CompilerParams(
            collective_id=1, has_side_effects=True, vmem_limit_bytes=VMEM_LIMIT
        ),
        name="layer",
    )(coords[0, 0].T, counts, features, weight, tiles[0, 0], cotangent)
    return pl.pallas_call(
        hand_over,
        out_shape=shapes,
        in_specs=[VM] * 3,
        out_specs=(VM,) * 3,
        name="hand_over",
    )(*results)


def solution(mesh):
    placed = (
        P(("col", "row"), None),
        P(),
        P("row", "col", None, None, None),
        P("row", "col", None, None),
        P("row", "col"),
        P(("row", "col"), None),
    )
    return jax.shard_map(
        body,
        mesh=mesh,
        in_specs=placed,
        out_specs=(P(("row", "col"), None), P(("col", "row"), None), P()),
        check_vma=False,
    )
```
